128 devices in a mesh: rep: 8 (over x, z_lo), tm: 4 (over y), space: 4 (over z_hi, core).
Axes of the slice: x: 4, y: 4, z: 4 (z_hi: 2, z_lo: 2; z = z_hi * 2 + z_lo), core: 2. Of those that a mesh axis runs over, the one named last changes fastest.
Arguments:
- query_spatial: bfloat16 [64, 384, 3072], P(('rep', 'tm'), 'space'), parts along dimension 0, may hold values from -16 to 16
- key_spatial: bfloat16 [64, 384, 3072], P(('rep', 'tm'), 'space'), parts along dimension 0, may hold values from -16 to 16
- value_spatial: bfloat16 [64, 384, 3072], P(('rep', 'tm'), 'space'), parts along dimension 0, may hold values from -6 to 6
- query_temporal: bfloat16 [64, 384, 3072], P(('rep', 'tm'), 'space'), parts along dimension 0, may hold values from -16 to 16
- key_temporal: bfloat16 [64, 384, 3072], P(('rep', 'tm'), 'space'), parts along dimension 0, may hold values from -16 to 16
- value_temporal: bfloat16 [64, 384, 3072], P(('rep', 'tm'), 'space'), parts along dimension 0, may hold values from -6 to 6
- upstream: bfloat16 [64, 384, 3072], P(('rep', 'tm'), 'space'), parts along dimension 0, may hold values from -36 to 36
- weight_spatial: bfloat16 [3072, 3072], P('space'), may hold values from -0.109375 to 0.109375
- weight_temporal: bfloat16 [3072, 3072], P('tm'), may hold values from -0.109375 to 0.109375
Outputs:
- grad_query_spatial: bfloat16 [64, 384, 3072], P(('rep', 'tm'), 'space'), parts along dimension 0
- grad_key_spatial: bfloat16 [64, 384, 3072], P(('rep', 'tm'), 'space'), parts along dimension 0
- grad_value_spatial: bfloat16 [64, 384, 3072], P(('rep', 'tm'), 'space'), parts along dimension 0
- grad_query_temporal: bfloat16 [64, 384, 3072], P(('rep', 'tm'), 'space'), parts along dimension 0
- grad_key_temporal: bfloat16 [64, 384, 3072], P(('rep', 'tm'), 'space'), parts along dimension 0
- grad_value_temporal: bfloat16 [64, 384, 3072], P(('rep', 'tm'), 'space'), parts along dimension 0
The draws below stay inside these ranges and needn't reach their ends.
There are 8 independent parts, one for each index of `rep`. The reference program is written for one: setup_inputs(seed, part) draws one part's arguments, and reference() takes and returns one part's arrays. A program takes and returns all parts, laid end to end along the dimension named above; an argument that names none is the same for every part. Nothing has to cross between parts.
All inputs are finite; a program needn't handle non-finite values.
Results may differ from the reference program's by a relative error of at most 0.0076.
Values may be sent and summed in bfloat16 or wider, within the bound.
A program may use at most 192 MiB of HBM per device.

```python
import math
import jax
import jax.numpy as jnp
from jax import lax

HEAD_DIM = 128
D = 3072
FRAMES = 8
TOKENS_FRAME = 384


def paired_fields(key, axis, salt, blend_weight):
    key = jax.random.fold_in(key, salt)
    key_query, key_keys, key_shared = jax.random.split(key, 3)
    shape = (FRAMES, TOKENS_FRAME, D)
    base_query = jnp.clip(jax.random.normal(key_query, shape, jnp.float32), -6.0, 6.0)
    base_keys = jnp.clip(jax.random.normal(key_keys, shape, jnp.float32), -6.0, 6.0)
    shared = jnp.clip(jax.random.normal(key_shared, shape, jnp.float32), -3.5, 3.5)
    row_index = jnp.arange(FRAMES)[:, None] * TOKENS_FRAME + jnp.arange(TOKENS_FRAME)[None, :]
    chosen = jnp.where(row_index % 37 == 3, blend_weight, 0.0).astype(jnp.float32)
    strength = 3.0 + 0.7 * (row_index // 37 % 3).astype(jnp.float32)
    aligned = strength[:, :, None] * shared
    query_field = base_query + chosen[:, :, None] * (aligned - base_query)
    key_field = base_keys + chosen[:, :, None] * (aligned - base_keys)
    near_weight = jnp.roll(chosen, 1, axis)
    near_strength = jnp.roll(strength, 1, axis)
    shrink = 1.0 - 2.0 / (near_strength * near_strength * math.sqrt(HEAD_DIM))
    near_value = jnp.roll(aligned, 1, axis) * shrink[:, :, None]
    key_field = key_field + near_weight[:, :, None] * (near_value - key_field)
    return (query_field, key_field)


def draw_query_spatial(key, part):
    blend_weight = 0.0
    return paired_fields(key, 1, 11, blend_weight)[0].astype(jnp.bfloat16)


def draw_key_spatial(key, part):
    blend_weight = 0.0
    return paired_fields(key, 1, 11, blend_weight)[1].astype(jnp.bfloat16)


def draw_query_temporal(key, part):
    blend_weight = 0.0
    return paired_fields(key, 0, 23, blend_weight)[0].astype(jnp.bfloat16)


def draw_key_temporal(key, part):
    blend_weight = 0.0
    return paired_fields(key, 0, 23, blend_weight)[1].astype(jnp.bfloat16)


def steps_of(rng, shape, pieces, smallest, top_value):
    factor_of = 1.0
    for position, shards_of in pieces:
        heights = jax.random.uniform(jax.random.fold_in(jax.random.fold_in(rng, 6), position), (shards_of,), jnp.float32, smallest / len(pieces), top_value / len(pieces))
        factor_of = factor_of * jnp.repeat(jnp.exp(heights), shape[position] // shards_of).reshape((-1,) + (1,) * (len(shape) - 1 - position))
    return factor_of


def centred(stream_key, dims, scale, most, cuts=(), dtype=jnp.bfloat16):
    result = jax.random.normal(stream_key, dims, jnp.float32) * scale
    if len(cuts) > 0:
        result = steps_of(stream_key, dims, cuts, -0.22, 0.18) * result
    return jnp.clip(result, min=-most, max=most).astype(dtype)


def setup_inputs(seed: int = 0, part: int = 0) -> dict:
    streams_of = jax.random.split(jax.random.key(seed), 10)
    part_splits = jax.random.split(jax.random.fold_in(streams_of[9], part), 10)
    return {
        "query_spatial": draw_query_spatial(jax.random.fold_in(jax.random.fold_in(streams_of[9], part), 71), part),
        "key_spatial": draw_key_spatial(jax.random.fold_in(jax.random.fold_in(streams_of[9], part), 71), part),
        "value_spatial": centred(part_splits[2], (FRAMES, TOKENS_FRAME, D), 1.0, 6.0, ((0, 4), (1, 4))),
        "query_temporal": draw_query_temporal(jax.random.fold_in(jax.random.fold_in(streams_of[9], part), 71), part),
        "key_temporal": draw_key_temporal(jax.random.fold_in(jax.random.fold_in(streams_of[9], part), 71), part),
        "value_temporal": centred(part_splits[5], (FRAMES, TOKENS_FRAME, D), 1.0, 6.0, ((0, 4), (1, 4))),
        "upstream": centred(part_splits[6], (FRAMES, TOKENS_FRAME, D), 6.0, 36.0, ((0, 4), (1, 4))),
        "weight_spatial": centred(streams_of[7], (D, D), D ** -0.5, 0.109375, ((0, 4),)),
        "weight_temporal": centred(streams_of[8], (D, D), D ** -0.5, 0.109375, ((0, 4),)),
    }


def attention_core(queries, key_rows, value_rows, out_grad, layout):
    key_layout = layout.replace("n", "m")
    scale = HEAD_DIM ** -0.5
    to_scores = layout + "," + key_layout + "->bhnm"
    scores = jnp.einsum(to_scores, queries.astype(jnp.float32), key_rows.astype(jnp.float32)) * scale
    attend = jax.nn.softmax(scores, axis=-1)
    attend_low = lax.optimization_barrier(attend.astype(jnp.bfloat16))
    grad_values = jnp.einsum("bhnm," + layout + "->" + key_layout, attend_low.astype(jnp.float32), out_grad.astype(jnp.float32))
    grad_attend = jnp.einsum(to_scores, out_grad.astype(jnp.float32), value_rows.astype(jnp.float32))
    grad_scores = attend * (grad_attend - jnp.sum(attend * grad_attend, axis=-1, keepdims=True))
    scaled_low = lax.optimization_barrier((grad_scores * scale).astype(jnp.bfloat16))
    grad_queries = jnp.einsum("bhnm," + key_layout + "->" + layout, scaled_low.astype(jnp.float32), key_rows.astype(jnp.float32))
    grad_keys = jnp.einsum("bhnm," + layout + "->" + key_layout, scaled_low.astype(jnp.float32), queries.astype(jnp.float32))
    return grad_queries.astype(jnp.bfloat16), grad_keys.astype(jnp.bfloat16), grad_values.astype(jnp.bfloat16)


def reference(query_spatial, key_spatial, value_spatial, query_temporal, key_temporal, value_temporal, upstream, weight_spatial, weight_temporal):
    frames, tokens, width = upstream.shape
    shape_heads = (frames, tokens, width // HEAD_DIM, HEAD_DIM)
    flat = upstream.reshape(frames * tokens, width)
    results = []
    blocks = ((weight_spatial, query_spatial, key_spatial, value_spatial, "bnhe"), (weight_temporal, query_temporal, key_temporal, value_temporal, "nbhe"))
    for weight, queries, key_rows, value_rows, layout in blocks:
        out_grad = jnp.dot(flat, weight.T, preferred_element_type=jnp.float32).astype(jnp.bfloat16).reshape(shape_heads)
        grads = attention_core(queries.reshape(shape_heads), key_rows.reshape(shape_heads), value_rows.reshape(shape_heads), out_grad, layout)
        for single in grads:
            results.append(single.reshape(frames, tokens, width))
    return (results[0], results[1], results[2], results[3], results[4], results[5])
```

```python
import functools

import jax
import jax.numpy as jnp
from jax import lax
from jax.experimental import pallas as pl
from jax.experimental.pallas import tpu as pltpu
from jax.sharding import PartitionSpec as P

HEAD = 128
SCALE = HEAD ** (-0.5)
MESH = pl.DeviceIdType.MESH
STEP = 16
BEFORE_SPATIAL = (2, 4)
NT = (((1,), (1,)), ((), ()))
NN = (((1,), (0,)), ((), ()))
TN = (((0,), (0,)), ((), ()))


def mul(a, b, dims):
    return lax.dot_general(a, b, dims, preferred_element_type=jnp.float32)


def attention(q, k, v, o, mask):
    scores = mul(k, q, NT) * SCALE
    if mask is not None:
        scores = jnp.where(mask, scores, -3.0e38)
    e = jnp.exp(scores - jnp.max(scores, axis=0, keepdims=True))
    a = e * (1.0 / jnp.sum(e, axis=0, keepdims=True))
    gv = mul(a.astype(jnp.bfloat16), o, NN)
    da = mul(v, o, NT)
    ds = a * (da - jnp.sum(a * da, axis=0, keepdims=True))
    low = (ds * SCALE).astype(jnp.bfloat16)
    gk = mul(low, q, NN)
    gq = mul(low, k, TN)
    return gq.astype(jnp.bfloat16), gk.astype(jnp.bfloat16), gv.astype(jnp.bfloat16)


def core(qs, ks, vs, qt, kt, vt, up, ws, wt, out,
         up_s, up_t, a_s, a_t, w_s, w_t, og_s, og_t, g_s, g_t,
         own_sem, upz_sem, qkvz_sem, upy_sem, qkvy_sem, gz_sem, gy_sem, send_sem):
    frames, rows, width = up.shape
    part = a_s.shape[-1]
    heads = part // HEAD
    steps = rows // STEP
    t = lax.axis_index("tm")
    s = lax.axis_index("space")
    n = 4
    y_up, y_down, y_far = lax.rem(t + 1, n), lax.rem(t + n - 1, n), lax.rem(t + 2, n)
    pair = s + 1 - 2 * lax.rem(s, 2)
    far = lax.rem(s + 2, n)
    cross = lax.rem(pair + 2, n)

    barrier = pltpu.get_barrier_semaphore()
    for d in (y_up, y_down, y_far):
        pl.semaphore_signal(barrier, inc=1, device_id={"tm": d}, device_id_type=MESH)
    for d in (pair, far, cross):
        pl.semaphore_signal(barrier, inc=1, device_id={"space": d}, device_id_type=MESH)

    def cols(d):
        return pl.ds(pl.multiple_of(d * part, part), part)

    def tokens(d):
        return pl.ds(pl.multiple_of(d * rows, rows), rows)

    def toks(i):
        return pl.ds(pl.multiple_of(i * STEP, STEP), STEP)

    def remote(src, dst, sem, **where):
        return pltpu.make_async_remote_copy(
            src, dst, send_sem.at[0], sem, device_id=where, device_id_type=MESH)

    def arrived(ref, sem):
        pltpu.make_async_copy(ref, ref, sem).wait()

    own = [
        pltpu.make_async_copy(up, up_t.at[pl.ds(2 * t, 2)], own_sem.at[0]),
        pltpu.make_async_copy(wt, w_t, own_sem.at[1]),
        pltpu.make_async_copy(up, up_s.at[:, tokens(s)], own_sem.at[2]),
        pltpu.make_async_copy(ws, w_s, own_sem.at[3]),
    ]
    for j, (src_t, src_s) in enumerate(((qt, qs), (kt, ks), (vt, vs))):
        own.append(pltpu.make_async_copy(src_t.at[:, :, cols(t)], a_t.at[j, pl.ds(2 * t, 2)], own_sem.at[4 + j]))
        own.append(pltpu.make_async_copy(src_s.at[:, :, cols(s)], a_s.at[j, :, tokens(s)], own_sem.at[7 + j]))
    for copy in own:
        copy.start()
    pl.semaphore_wait(barrier, 6)

    def send_space(f):
        for d, slot in ((far, 0), (pair, 1)):
            remote(up.at[f], up_s.at[f, tokens(s)], upz_sem.at[f, slot], space=d).start()
        for j, src in enumerate((qs, ks, vs)):
            for d in (far, cross, pair):
                remote(src.at[f, :, cols(d)], a_s.at[j, f, tokens(s)], qkvz_sem.at[f], space=d).start()

    def send_time(i):
        for d, slot in ((y_up, 0), (y_down, 1)):
            remote(up.at[:, toks(i)], up_t.at[pl.ds(2 * t, 2), toks(i)], upy_sem.at[i, slot], tm=d).start()
        for j, src in enumerate((qt, kt, vt)):
            for d in (y_up, y_down, y_far):
                remote(src.at[:, toks(i), cols(d)], a_t.at[j, pl.ds(2 * t, 2), toks(i)], qkvy_sem.at[i], tm=d).start()

    def pass_time(i):
        arrived(up_t.at[pl.ds(0, 2), toks(i)], upy_sem.at[i, 0])
        low = 2 * y_down
        remote(up_t.at[low, toks(i)], up_t.at[low, toks(i)], upy_sem.at[i, 2], tm=y_up).start()
        arrived(up_t.at[pl.ds(0, 2), toks(i)], upy_sem.at[i, 1])
        high = 2 * y_up + 1
        remote(up_t.at[high, toks(i)], up_t.at[high, toks(i)], upy_sem.at[i, 3], tm=y_down).start()

    def finish_time(i):
        arrived(up_t.at[0, toks(i)], upy_sem.at[i, 2])
        arrived(up_t.at[0, toks(i)], upy_sem.at[i, 3])
        arrived(a_t.at[:, pl.ds(0, 6), toks(i)], qkvy_sem.at[i])

    def time_step(i):
        x = up_t[:, toks(i), :].reshape(8 * STEP, width)
        og_t[...] = mul(x, w_t[...], NT).astype(jnp.bfloat16)
        size = 8 * STEP
        mask = (lax.broadcasted_iota(jnp.int32, (size, size), 0) % STEP
                == lax.broadcasted_iota(jnp.int32, (size, size), 1) % STEP)
        for h in range(heads):
            c = slice(h * HEAD, (h + 1) * HEAD)
            q, k, v = (a_t[j, :, toks(i), c].reshape(size, HEAD) for j in range(3))
            for j, g in enumerate(attention(q, k, v, og_t[:, c], mask)):
                g_t[j, :, toks(i), c] = g.reshape(8, STEP, HEAD)
        pltpu.make_async_copy(g_t.at[:, pl.ds(2 * t, 2), toks(i)], out.at[pl.ds(3, 3), :, toks(i), cols(t)], gy_sem.at[1]).start()
        for d in (y_far, y_up, y_down):
            remote(g_t.at[:, pl.ds(2 * d, 2), toks(i)], out.at[pl.ds(3, 3), :, toks(i), cols(t)], gy_sem.at[0], tm=d).start()

    def space_part(f):
        arrived(up_s.at[f, pl.ds(0, rows)], upz_sem.at[f, 0])
        remote(up_s.at[f, tokens(far)], up_s.at[f, tokens(far)], upz_sem.at[f, 2], space=pair).start()
        arrived(up_s.at[f, pl.ds(0, rows)], upz_sem.at[f, 1])
        arrived(up_s.at[f, pl.ds(0, rows)], upz_sem.at[f, 2])
        arrived(a_s.at[:, f, pl.ds(0, 3 * rows)], qkvz_sem.at[f])
        og_s[...] = mul(up_s[f], w_s[...], NT).astype(jnp.bfloat16)

        def head(h, carry):
            c = pl.ds(pl.multiple_of(h * HEAD, HEAD), HEAD)
            q, k, v = (a_s[j, f, :, c] for j in range(3))
            for j, g in enumerate(attention(q, k, v, og_s[:, c], None)):
                g_s[j, f, :, c] = g
            return carry

        half = heads // 2
        for b in range(2):
            lax.fori_loop(b * half, (b + 1) * half, head, 0)
            here = pl.ds(b * half * HEAD, half * HEAD)
            there = pl.ds(pl.multiple_of(s * part + b * half * HEAD, HEAD), half * HEAD)
            pltpu.make_async_copy(g_s.at[:, f, tokens(s), here], out.at[pl.ds(0, 3), f, :, there], gz_sem.at[1]).start()
            for d in (far, cross, pair):
                remote(g_s.at[:, f, tokens(d), here], out.at[pl.ds(0, 3), f, :, there], gz_sem.at[0], space=d).start()

    send_space(0)
    for i in range(steps):
        send_time(i)
        if i == 2:
            send_space(1)
    pass_time(0)
    for copy in own:
        copy.wait()

    def step(i, carry):
        @pl.when(i + 1 < steps)
        def _():
            pass_time(i + 1)

        finish_time(i)
        time_step(i)

        @pl.when((i == BEFORE_SPATIAL[0]) | (i == BEFORE_SPATIAL[1]))
        def _():
            space_part(jnp.where(i == BEFORE_SPATIAL[0], 0, 1))
        return carry

    lax.fori_loop(0, steps, step, 0)

    arrived(out.at[pl.ds(0, 3), :, :, pl.ds(0, part)], gz_sem.at[1])
    arrived(out.at[pl.ds(0, 3), :, :, pl.ds(0, 3 * part)], gz_sem.at[0])
    arrived(out.at[pl.ds(3, 3), :, :, pl.ds(0, part)], gy_sem.at[1])
    arrived(out.at[pl.ds(3, 3), :, :, pl.ds(0, 3 * part)], gy_sem.at[0])
    for _ in range(6):
        arrived(up_t.at[pl.ds(0, 2)], send_sem.at[0])
    for ref in (a_s.at[:, :, pl.ds(0, 3 * rows)], a_t.at[:, pl.ds(0, 6)]):
        arrived(ref, send_sem.at[0])
        arrived(ref, send_sem.at[0])


def split(whole, *rest):
    outs, sem = rest[:-1], rest[-1]
    copies = [pltpu.make_async_copy(whole.at[j], o, sem.at[j]) for j, o in enumerate(outs)]
    for copy in copies:
        copy.start()
    for copy in copies:
        copy.wait()


def local(*args):
    up, ws = args[6], args[7]
    frames, rows, width = up.shape
    part = ws.shape[0]
    bf = jnp.bfloat16
    anywhere = pl.BlockSpec(memory_space=pl.ANY)
    whole = pl.pallas_call(
        core,
        out_shape=jax.ShapeDtypeStruct((6, frames, rows, width), bf),
        in_specs=[anywhere] * 9,
        out_specs=anywhere,
        scratch_shapes=[
            pltpu.VMEM((frames, 4 * rows, width), bf),
            pltpu.VMEM((4 * frames, rows, width), bf),
            pltpu.VMEM((3, frames, 4 * rows, part), bf),
            pltpu.VMEM((3, 4 * frames, rows, part), bf),
            pltpu.VMEM((part, width), bf),
            pltpu.VMEM((part, width), bf),
            pltpu.VMEM((4 * rows, part), bf),
            pltpu.VMEM((4 * frames * STEP, part), bf),
            pltpu.VMEM((3, frames, 4 * rows, part), bf),
            pltpu.VMEM((3, 4 * frames, rows, part), bf),
            pltpu.SemaphoreType.DMA((10,)),
            pltpu.SemaphoreType.DMA((frames, 3)),
            pltpu.SemaphoreType.DMA((frames,)),
            pltpu.SemaphoreType.DMA((rows // STEP, 4)),
            pltpu.SemaphoreType.DMA((rows // STEP,)),
            pltpu.SemaphoreType.DMA((2,)),
            pltpu.SemaphoreType.DMA((2,)),
            pltpu.SemaphoreType.DMA((1,)),
        ],
        compiler_params=pltpu.CompilerParams(
            collective_id=0, has_side_effects=True, vmem_limit_bytes=56 * 1024 * 1024),
        name="core",
    )(*args)
    one = jax.ShapeDtypeStruct((frames, rows, width), bf)
    return tuple(pl.pallas_call(
        split,
        out_shape=[one] * 6,
        in_specs=[anywhere],
        out_specs=[anywhere] * 6,
        scratch_shapes=[pltpu.SemaphoreType.DMA((6,))],
        name="split",
    )(whole))


def solution(mesh):
    rows = P(("rep", "tm"), "space", None)
    in_specs = (rows,) * 7 + (P("space", None), P("tm", None))
    return jax.shard_map(local, mesh=mesh, in_specs=in_specs, out_specs=(rows,) * 6, check_vma=False)
```

```python
import jax
import jax.numpy as jnp
from jax import lax
from jax.experimental import pallas as pl
from jax.experimental.pallas import tpu as pltpu
from jax.sharding import PartitionSpec as P

HEAD = 128
SCALE = HEAD ** (-0.5)
MESH = pl.DeviceIdType.MESH
STEP = 16
BEFORE_SPATIAL = (2, 4)
NT = (((1,), (1,)), ((), ()))
NN = (((1,), (0,)), ((), ()))
TN = (((0,), (0,)), ((), ()))


def mul(a, b, dims):
    return lax.dot_general(a, b, dims, preferred_element_type=jnp.float32)


def attention(q, k, v, o, mask):
    scores = mul(k, q, NT) * SCALE
    if mask is not None:
        scores = jnp.where(mask, scores, -3.0e38)
    e = jnp.exp(scores - jnp.max(scores, axis=0, keepdims=True))
    a = e * (1.0 / jnp.sum(e, axis=0, keepdims=True))
    gv = mul(a.astype(jnp.bfloat16), o, NN)
    da = mul(v, o, NT)
    ds = a * (da - jnp.sum(a * da, axis=0, keepdims=True))
    low = (ds * SCALE).astype(jnp.bfloat16)
    gk = mul(low, q, NN)
    gq = mul(low, k, TN)
    return gq.astype(jnp.bfloat16), gk.astype(jnp.bfloat16), gv.astype(jnp.bfloat16)


def core(qs, ks, vs, qt, kt, vt, up, ws, wt, out,
         up_s, up_t, a_s, a_t, w_s, w_t, og_s, og_t, g_s, g_t,
         own_sem, upz_sem, qkvz_sem, upy_sem, qkvy_sem, gz_sem, gy_sem, send_sem):
    frames, rows, width = up.shape
    part = a_s.shape[-1]
    heads = part // HEAD
    steps = rows // STEP
    t = lax.axis_index("tm")
    s = lax.axis_index("space")
    n = 4
    y_up, y_down, y_far = lax.rem(t + 1, n), lax.rem(t + n - 1, n), lax.rem(t + 2, n)
    pair = s + 1 - 2 * lax.rem(s, 2)
    far = lax.rem(s + 2, n)
    cross = lax.rem(pair + 2, n)

    barrier = pltpu.get_barrier_semaphore()
    for d in (y_up, y_down, y_far):
        pl.semaphore_signal(barrier, inc=1, device_id={"tm": d}, device_id_type=MESH)
    for d in (pair, far, cross):
        pl.semaphore_signal(barrier, inc=1, device_id={"space": d}, device_id_type=MESH)

    def cols(d):
        return pl.ds(pl.multiple_of(d * part, part), part)

    def tokens(d):
        return pl.ds(pl.multiple_of(d * rows, rows), rows)

    def toks(i):
        return pl.ds(pl.multiple_of(i * STEP, STEP), STEP)

    def remote(src, dst, sem, **where):
        return pltpu.make_async_remote_copy(
            src, dst, send_sem.at[0], sem, device_id=where, device_id_type=MESH)

    def arrived(ref, sem):
        pltpu.make_async_copy(ref, ref, sem).wait()

    own = [
        pltpu.make_async_copy(up, up_t.at[pl.ds(2 * t, 2)], own_sem.at[0]),
        pltpu.make_async_copy(wt, w_t, own_sem.at[1]),
        pltpu.make_async_copy(up, up_s.at[:, tokens(s)], own_sem.at[2]),
        pltpu.make_async_copy(ws, w_s, own_sem.at[3]),
    ]
    for j, (src_t, src_s) in enumerate(((qt, qs), (kt, ks), (vt, vs))):
        own.append(pltpu.make_async_copy(src_t.at[:, :, cols(t)], a_t.at[j, pl.ds(2 * t, 2)], own_sem.at[4 + j]))
        own.append(pltpu.make_async_copy(src_s.at[:, :, cols(s)], a_s.at[j, :, tokens(s)], own_sem.at[7 + j]))
    for copy in own:
        copy.start()
    pl.semaphore_wait(barrier, 6)

    def send_space(f):
        for d, slot in ((far, 0), (pair, 1)):
            remote(up.at[f], up_s.at[f, tokens(s)], upz_sem.at[f, slot], space=d).start()
        for j, src in enumerate((qs, ks, vs)):
            for d in (far, cross, pair):
                remote(src.at[f, :, cols(d)], a_s.at[j, f, tokens(s)], qkvz_sem.at[f], space=d).start()

    def send_time(i):
        for d, slot in ((y_up, 0), (y_down, 1)):
            remote(up.at[:, toks(i)], up_t.at[pl.ds(2 * t, 2), toks(i)], upy_sem.at[i, slot], tm=d).start()
        for j, src in enumerate((qt, kt, vt)):
            for d in (y_up, y_down, y_far):
                remote(src.at[:, toks(i), cols(d)], a_t.at[j, pl.ds(2 * t, 2), toks(i)], qkvy_sem.at[i], tm=d).start()

    def pass_time(i):
        arrived(up_t.at[pl.ds(0, 2), toks(i)], upy_sem.at[i, 0])
        low = 2 * y_down
        remote(up_t.at[low, toks(i)], up_t.at[low, toks(i)], upy_sem.at[i, 2], tm=y_up).start()
        arrived(up_t.at[pl.ds(0, 2), toks(i)], upy_sem.at[i, 1])
        high = 2 * y_up + 1
        remote(up_t.at[high, toks(i)], up_t.at[high, toks(i)], upy_sem.at[i, 3], tm=y_down).start()

    def finish_time(i):
        arrived(up_t.at[0, toks(i)], upy_sem.at[i, 2])
        arrived(up_t.at[0, toks(i)], upy_sem.at[i, 3])
        arrived(a_t.at[:, pl.ds(0, 6), toks(i)], qkvy_sem.at[i])

    def time_step(i):
        x = up_t[:, toks(i), :].reshape(8 * STEP, width)
        og_t[...] = mul(x, w_t[...], NT).astype(jnp.bfloat16)
        size = 8 * STEP
        mask = (lax.broadcasted_iota(jnp.int32, (size, size), 0) % STEP
                == lax.broadcasted_iota(jnp.int32, (size, size), 1) % STEP)
        for h in range(heads):
            c = slice(h * HEAD, (h + 1) * HEAD)
            q, k, v = (a_t[j, :, toks(i), c].reshape(size, HEAD) for j in range(3))
            for j, g in enumerate(attention(q, k, v, og_t[:, c], mask)):
                g_t[j, :, toks(i), c] = g.reshape(8, STEP, HEAD)
        pltpu.make_async_copy(g_t.at[:, pl.ds(2 * t, 2), toks(i)], out.at[pl.ds(3, 3), :, toks(i), cols(t)], gy_sem.at[1]).start()
        for d in (y_far, y_up, y_down):
            remote(g_t.at[:, pl.ds(2 * d, 2), toks(i)], out.at[pl.ds(3, 3), :, toks(i), cols(t)], gy_sem.at[0], tm=d).start()

    def space_part(f):
        arrived(up_s.at[f, pl.ds(0, rows)], upz_sem.at[f, 0])
        remote(up_s.at[f, tokens(far)], up_s.at[f, tokens(far)], upz_sem.at[f, 2], space=pair).start()
        arrived(up_s.at[f, pl.ds(0, rows)], upz_sem.at[f, 1])
        arrived(up_s.at[f, pl.ds(0, rows)], upz_sem.at[f, 2])
        arrived(a_s.at[:, f, pl.ds(0, 3 * rows)], qkvz_sem.at[f])
        og_s[...] = mul(up_s[f], w_s[...], NT).astype(jnp.bfloat16)

        def head(h, carry):
            c = pl.ds(pl.multiple_of(h * HEAD, HEAD), HEAD)
            q, k, v = (a_s[j, f, :, c] for j in range(3))
            for j, g in enumerate(attention(q, k, v, og_s[:, c], None)):
                g_s[j, f, :, c] = g
            return carry

        half = heads // 2
        for b in range(2):
            lax.fori_loop(b * half, (b + 1) * half, head, 0)
            here = pl.ds(b * half * HEAD, half * HEAD)
            there = pl.ds(pl.multiple_of(s * part + b * half * HEAD, HEAD), half * HEAD)
            pltpu.make_async_copy(g_s.at[:, f, tokens(s), here], out.at[pl.ds(0, 3), f, :, there], gz_sem.at[1]).start()
            for d in (far, cross, pair):
                remote(g_s.at[:, f, tokens(d), here], out.at[pl.ds(0, 3), f, :, there], gz_sem.at[0], space=d).start()

    send_space(0)
    for i in range(2):
        send_time(i)
    send_space(1)
    pass_time(0)
    for copy in own:
        copy.wait()

    def step(i, carry):
        @pl.when(i + 1 < steps)
        def _():
            pass_time(i + 1)

        @pl.when(i + 2 < steps)
        def _():
            send_time(i + 2)

        finish_time(i)
        time_step(i)

        @pl.when((i == BEFORE_SPATIAL[0]) | (i == BEFORE_SPATIAL[1]))
        def _():
            space_part(jnp.where(i == BEFORE_SPATIAL[0], 0, 1))
        return carry

    lax.fori_loop(0, steps, step, 0)

    arrived(out.at[pl.ds(0, 3), :, :, pl.ds(0, part)], gz_sem.at[1])
    arrived(out.at[pl.ds(0, 3), :, :, pl.ds(0, 3 * part)], gz_sem.at[0])
    arrived(out.at[pl.ds(3, 3), :, :, pl.ds(0, part)], gy_sem.at[1])
    arrived(out.at[pl.ds(3, 3), :, :, pl.ds(0, 3 * part)], gy_sem.at[0])
    for _ in range(6):
        arrived(up_t.at[pl.ds(0, 2)], send_sem.at[0])
    for ref in (a_s.at[:, :, pl.ds(0, 3 * rows)], a_t.at[:, pl.ds(0, 6)]):
        arrived(ref, send_sem.at[0])
        arrived(ref, send_sem.at[0])


def local(*args):
    up, ws = args[6], args[7]
    frames, rows, width = up.shape
    part = ws.shape[0]
    bf = jnp.bfloat16
    anywhere = pl.BlockSpec(memory_space=pl.ANY)
    whole = pl.pallas_call(
        core,
        out_shape=pltpu.VMEM((6, frames, rows, width), bf),
        in_specs=[pl.BlockSpec(memory_space=pltpu.HBM)] * 9,
        out_specs=pl.BlockSpec(memory_space=pltpu.VMEM),
        scratch_shapes=[
            pltpu.VMEM((frames, 4 * rows, width), bf),
            pltpu.VMEM((4 * frames, rows, width), bf),
            pltpu.VMEM((3, frames, 4 * rows, part), bf),
            pltpu.VMEM((3, 4 * frames, rows, part), bf),
            pltpu.VMEM((part, width), bf),
            pltpu.VMEM((part, width), bf),
            pltpu.VMEM((4 * rows, part), bf),
            pltpu.VMEM((4 * frames * STEP, part), bf),
            pltpu.VMEM((3, frames, 4 * rows, part), bf),
            pltpu.VMEM((3, 4 * frames, rows, part), bf),
            pltpu.SemaphoreType.DMA((10,)),
            pltpu.SemaphoreType.DMA((frames, 3)),
            pltpu.SemaphoreType.DMA((frames,)),
            pltpu.SemaphoreType.DMA((rows // STEP, 4)),
            pltpu.SemaphoreType.DMA((rows // STEP,)),
            pltpu.SemaphoreType.DMA((2,)),
            pltpu.SemaphoreType.DMA((2,)),
            pltpu.SemaphoreType.DMA((1,)),
        ],
        compiler_params=pltpu.CompilerParams(
            collective_id=0, has_side_effects=True, vmem_limit_bytes=57 * 1024 * 1024),
        name="core",
    )(*args)
    return tuple(whole[j] for j in range(6))


def solution(mesh):
    rows = P(("rep", "tm"), "space", None)
    in_specs = (rows,) * 7 + (P("space", None), P("tm", None))
    return jax.shard_map(local, mesh=mesh, in_specs=in_specs, out_specs=(rows,) * 6, check_vma=False)
```

```python
import jax
import jax.numpy as jnp
from jax import lax
from jax.experimental import pallas as pl
from jax.experimental.pallas import tpu as pltpu
from jax.sharding import PartitionSpec as P

HEAD = 128
SCALE = HEAD ** (-0.5)
MESH = pl.DeviceIdType.MESH
STEP = 16
BEFORE_SPATIAL = (1, 3)
NT = (((1,), (1,)), ((), ()))
NN = (((1,), (0,)), ((), ()))
TN = (((0,), (0,)), ((), ()))


def mul(a, b, dims):
    return lax.dot_general(a, b, dims, preferred_element_type=jnp.float32)


def attention(q, k, v, o, mask):
    scores = mul(k, q, NT) * SCALE
    if mask is not None:
        scores = jnp.where(mask, scores, -3.0e38)
    e = jnp.exp(scores - jnp.max(scores, axis=0, keepdims=True))
    a = e * (1.0 / jnp.sum(e, axis=0, keepdims=True))
    gv = mul(a.astype(jnp.bfloat16), o, NN)
    da = mul(v, o, NT)
    ds = a * (da - jnp.sum(a * da, axis=0, keepdims=True))
    low = (ds * SCALE).astype(jnp.bfloat16)
    gk = mul(low, q, NN)
    gq = mul(low, k, TN)
    return gq.astype(jnp.bfloat16), gk.astype(jnp.bfloat16), gv.astype(jnp.bfloat16)


def core(qs, ks, vs, qt, kt, vt, up, ws, wt, out,
         up_s, up_t, a_s, a_t, w_s, w_t, og_s, og_t, g_s, g_t,
         own_sem, upz_sem, qkvz_sem, upy_sem, qkvy_sem, gz_sem, gy_sem, send_sem):
    frames, rows, width = up.shape
    part = a_s.shape[-1]
    heads = part // HEAD
    steps = rows // STEP
    t = lax.axis_index("tm")
    s = lax.axis_index("space")
    n = 4
    y_up, y_down, y_far = lax.rem(t + 1, n), lax.rem(t + n - 1, n), lax.rem(t + 2, n)
    pair = s + 1 - 2 * lax.rem(s, 2)
    far = lax.rem(s + 2, n)
    cross = lax.rem(pair + 2, n)

    barrier = pltpu.get_barrier_semaphore()
    for d in (y_up, y_down, y_far):
        pl.semaphore_signal(barrier, inc=1, device_id={"tm": d}, device_id_type=MESH)
    for d in (pair, far, cross):
        pl.semaphore_signal(barrier, inc=1, device_id={"space": d}, device_id_type=MESH)

    def cols(d):
        return pl.ds(pl.multiple_of(d * part, part), part)

    def tokens(d):
        return pl.ds(pl.multiple_of(d * rows, rows), rows)

    def toks(i):
        return pl.ds(pl.multiple_of(i * STEP, STEP), STEP)

    def remote(src, dst, sem, **where):
        return pltpu.make_async_remote_copy(
            src, dst, send_sem.at[0], sem, device_id=where, device_id_type=MESH)

    def arrived(ref, sem):
        pltpu.make_async_copy(ref, ref, sem).wait()

    own = [
        pltpu.make_async_copy(up, up_t.at[pl.ds(2 * t, 2)], own_sem.at[0]),
        pltpu.make_async_copy(wt, w_t, own_sem.at[1]),
        pltpu.make_async_copy(up, up_s.at[:, tokens(s)], own_sem.at[2]),
        pltpu.make_async_copy(ws, w_s, own_sem.at[3]),
    ]
    for j, (src_t, src_s) in enumerate(((qt, qs), (kt, ks), (vt, vs))):
        own.append(pltpu.make_async_copy(src_t.at[:, :, cols(t)], a_t.at[j, pl.ds(2 * t, 2)], own_sem.at[4 + j]))
        own.append(pltpu.make_async_copy(src_s.at[:, :, cols(s)], a_s.at[j, :, tokens(s)], own_sem.at[7 + j]))
    for copy in own:
        copy.start()
    pl.semaphore_wait(barrier, 6)

    def send_space(f):
        for d, slot in ((far, 0), (pair, 1)):
            remote(up.at[f], up_s.at[f, tokens(s)], upz_sem.at[f, slot], space=d).start()
        for j, src in enumerate((qs, ks, vs)):
            for d in (far, cross, pair):
                remote(src.at[f, :, cols(d)], a_s.at[j, f, tokens(s)], qkvz_sem.at[f], space=d).start()

    def send_time(i):
        for d, slot in ((y_up, 0), (y_down, 1)):
            remote(up.at[:, toks(i)], up_t.at[pl.ds(2 * t, 2), toks(i)], upy_sem.at[i, slot], tm=d).start()
        for j, src in enumerate((qt, kt, vt)):
            for d in (y_up, y_down, y_far):
                remote(src.at[:, toks(i), cols(d)], a_t.at[j, pl.ds(2 * t, 2), toks(i)], qkvy_sem.at[i], tm=d).start()

    def pass_time(i):
        arrived(up_t.at[pl.ds(0, 2), toks(i)], upy_sem.at[i, 0])
        low = 2 * y_down
        remote(up_t.at[low, toks(i)], up_t.at[low, toks(i)], upy_sem.at[i, 2], tm=y_up).start()
        arrived(up_t.at[pl.ds(0, 2), toks(i)], upy_sem.at[i, 1])
        high = 2 * y_up + 1
        remote(up_t.at[high, toks(i)], up_t.at[high, toks(i)], upy_sem.at[i, 3], tm=y_down).start()

    def finish_time(i):
        arrived(up_t.at[0, toks(i)], upy_sem.at[i, 2])
        arrived(up_t.at[0, toks(i)], upy_sem.at[i, 3])
        arrived(a_t.at[:, pl.ds(0, 6), toks(i)], qkvy_sem.at[i])

    def time_step(i):
        x = up_t[:, toks(i), :].reshape(8 * STEP, width)
        og_t[...] = mul(x, w_t[...], NT).astype(jnp.bfloat16)
        size = 8 * STEP
        mask = (lax.broadcasted_iota(jnp.int32, (size, size), 0) % STEP
                == lax.broadcasted_iota(jnp.int32, (size, size), 1) % STEP)
        for h in range(heads):
            c = slice(h * HEAD, (h + 1) * HEAD)
            q, k, v = (a_t[j, :, toks(i), c].reshape(size, HEAD) for j in range(3))
            for j, g in enumerate(attention(q, k, v, og_t[:, c], mask)):
                g_t[j, :, toks(i), c] = g.reshape(8, STEP, HEAD)
        for d in (y_far, y_up, y_down):
            remote(g_t.at[:, pl.ds(2 * d, 2), toks(i)], out.at[pl.ds(3, 3), :, toks(i), cols(t)], gy_sem.at[0], tm=d).start()
        pltpu.make_async_copy(g_t.at[:, pl.ds(2 * t, 2), toks(i)], out.at[pl.ds(3, 3), :, toks(i), cols(t)], gy_sem.at[1]).start()

    def space_part(f):
        arrived(up_s.at[f, pl.ds(0, rows)], upz_sem.at[f, 0])
        remote(up_s.at[f, tokens(far)], up_s.at[f, tokens(far)], upz_sem.at[f, 2], space=pair).start()
        arrived(up_s.at[f, pl.ds(0, rows)], upz_sem.at[f, 1])
        arrived(up_s.at[f, pl.ds(0, rows)], upz_sem.at[f, 2])
        arrived(a_s.at[:, f, pl.ds(0, 3 * rows)], qkvz_sem.at[f])
        og_s[...] = mul(up_s[f], w_s[...], NT).astype(jnp.bfloat16)

        def head(h, carry):
            c = pl.ds(pl.multiple_of(h * HEAD, HEAD), HEAD)
            q, k, v = (a_s[j, f, :, c] for j in range(3))
            for j, g in enumerate(attention(q, k, v, og_s[:, c], None)):
                g_s[j, f, :, c] = g
            return carry

        half = heads // 2
        for b in range(2):
            lax.fori_loop(b * half, (b + 1) * half, head, 0)
            here = pl.ds(b * half * HEAD, half * HEAD)
            there = pl.ds(pl.multiple_of(s * part + b * half * HEAD, HEAD), half * HEAD)
            for d in (far, cross, pair):
                remote(g_s.at[:, f, tokens(d), here], out.at[pl.ds(0, 3), f, :, there], gz_sem.at[0], space=d).start()
            pltpu.make_async_copy(g_s.at[:, f, tokens(s), here], out.at[pl.ds(0, 3), f, :, there], gz_sem.at[1]).start()

    send_time(0)
    send_space(0)
    send_time(1)
    send_space(1)
    pass_time(0)
    for copy in own:
        copy.wait()

    def step(i, carry):
        @pl.when(i + 1 < steps)
        def _():
            pass_time(i + 1)

        @pl.when(i + 2 < steps)
        def _():
            send_time(i + 2)

        finish_time(i)
        time_step(i)

        @pl.when((i == BEFORE_SPATIAL[0]) | (i == BEFORE_SPATIAL[1]))
        def _():
            space_part(jnp.where(i == BEFORE_SPATIAL[0], 0, 1))
        return carry

    lax.fori_loop(0, steps, step, 0)

    arrived(out.at[pl.ds(0, 3), :, :, pl.ds(0, part)], gz_sem.at[1])
    arrived(out.at[pl.ds(0, 3), :, :, pl.ds(0, 3 * part)], gz_sem.at[0])
    arrived(out.at[pl.ds(3, 3), :, :, pl.ds(0, part)], gy_sem.at[1])
    arrived(out.at[pl.ds(3, 3), :, :, pl.ds(0, 3 * part)], gy_sem.at[0])
    for _ in range(6):
        arrived(up_t.at[pl.ds(0, 2)], send_sem.at[0])
    for ref in (a_s.at[:, :, pl.ds(0, 3 * rows)], a_t.at[:, pl.ds(0, 6)]):
        arrived(ref, send_sem.at[0])
        arrived(ref, send_sem.at[0])


def local(*args):
    up, ws = args[6], args[7]
    frames, rows, width = up.shape
    part = ws.shape[0]
    bf = jnp.bfloat16
    anywhere = pl.BlockSpec(memory_space=pl.ANY)
    whole = pl.pallas_call(
        core,
        out_shape=pltpu.VMEM((6, frames, rows, width), bf),
        in_specs=[pl.BlockSpec(memory_space=pltpu.HBM)] * 9,
        out_specs=pl.BlockSpec(memory_space=pltpu.VMEM),
        scratch_shapes=[
            pltpu.VMEM((frames, 4 * rows, width), bf),
            pltpu.VMEM((4 * frames, rows, width), bf),
            pltpu.VMEM((3, frames, 4 * rows, part), bf),
            pltpu.VMEM((3, 4 * frames, rows, part), bf),
            pltpu.VMEM((part, width), bf),
            pltpu.VMEM((part, width), bf),
            pltpu.VMEM((4 * rows, part), bf),
            pltpu.VMEM((4 * frames * STEP, part), bf),
            pltpu.VMEM((3, frames, 4 * rows, part), bf),
            pltpu.VMEM((3, 4 * frames, rows, part), bf),
            pltpu.SemaphoreType.DMA((10,)),
            pltpu.SemaphoreType.DMA((frames, 3)),
            pltpu.SemaphoreType.DMA((frames,)),
            pltpu.SemaphoreType.DMA((rows // STEP, 4)),
            pltpu.SemaphoreType.DMA((rows // STEP,)),
            pltpu.SemaphoreType.DMA((2,)),
            pltpu.SemaphoreType.DMA((2,)),
            pltpu.SemaphoreType.DMA((1,)),
        ],
        compiler_params=pltpu.CompilerParams(
            collective_id=0, has_side_effects=True, vmem_limit_bytes=57 * 1024 * 1024),
        name="core",
    )(*args)
    return tuple(whole[j] for j in range(6))


def solution(mesh):
    rows = P(("rep", "tm"), "space", None)
    in_specs = (rows,) * 7 + (P("space", None), P("tm", None))
    return jax.shard_map(local, mesh=mesh, in_specs=in_specs, out_specs=(rows,) * 6, check_vma=False)
```

```python
import jax
import jax.numpy as jnp
from jax import lax
from jax.experimental import pallas as pl
from jax.experimental.pallas import tpu as pltpu
from jax.sharding import PartitionSpec as P

HEAD = 128
SCALE = HEAD ** (-0.5)
MESH = pl.DeviceIdType.MESH
STEP = 16
SPATIAL_AFTER = 1
PIECES = 2
NT = (((1,), (1,)), ((), ()))
NN = (((1,), (0,)), ((), ()))
TN = (((0,), (0,)), ((), ()))


def mul(a, b, dims):
    return lax.dot_general(a, b, dims, preferred_element_type=jnp.float32)


def attention(q, k, v, o, mask):
    scores = mul(k, q, NT) * SCALE
    if mask is not None:
        scores = jnp.where(mask, scores, -3.0e38)
    e = jnp.exp(scores - jnp.max(scores, axis=0, keepdims=True))
    a = e * (1.0 / jnp.sum(e, axis=0, keepdims=True))
    gv = mul(a.astype(jnp.bfloat16), o, NN)
    da = mul(v, o, NT)
    ds = a * (da - jnp.sum(a * da, axis=0, keepdims=True))
    low = (ds * SCALE).astype(jnp.bfloat16)
    gk = mul(low, q, NN)
    gq = mul(low, k, TN)
    return gq.astype(jnp.bfloat16), gk.astype(jnp.bfloat16), gv.astype(jnp.bfloat16)


def core(qs, ks, vs, qt, kt, vt, up, ws, wt, out,
         up_s, up_t, a_s, a_t, w_s, w_t, w_p, og_s, og_t, og_p, g_s, g_t,
         own_sem, upz_sem, qkvz_sem, upy_sem, qkvy_sem, ogy_sem, wy_sem, wx_sem, wc_sem, gz_sem, gy_sem, send_sem):
    frames, rows, width = up.shape
    part = a_s.shape[-1]
    heads = part // HEAD
    steps = rows // STEP
    r = lax.axis_index("rep")
    t = lax.axis_index("tm")
    s = lax.axis_index("space")
    n = 4
    x = r // 2
    core_id = lax.rem(s, 2)
    y_up, y_down, y_far = lax.rem(t + 1, n), lax.rem(t + n - 1, n), lax.rem(t + 2, n)
    mate = t + 1 - 2 * lax.rem(t, 2)
    mirror = n - 1 - t
    pair = s + 1 - 2 * core_id
    far = lax.rem(s + 2, n)
    cross = lax.rem(pair + 2, n)
    x_others = [lax.rem(x + k, n) * 2 + lax.rem(r, 2) for k in (1, 3, 2)]

    barrier = pltpu.get_barrier_semaphore()
    for d in (y_up, y_down, y_far):
        pl.semaphore_signal(barrier, inc=1, device_id={"tm": d}, device_id_type=MESH)
    for d in (pair, far, cross):
        pl.semaphore_signal(barrier, inc=1, device_id={"space": d}, device_id_type=MESH)
    for d in x_others:
        pl.semaphore_signal(barrier, inc=1, device_id={"rep": d}, device_id_type=MESH)

    def cols(d):
        return pl.ds(pl.multiple_of(d * part, part), part)

    def tokens(d):
        return pl.ds(pl.multiple_of(d * rows, rows), rows)

    def toks(i):
        return pl.ds(pl.multiple_of(i * STEP, STEP), STEP)

    def remote(src, dst, sem, **where):
        return pltpu.make_async_remote_copy(
            src, dst, send_sem.at[0], sem, device_id=where, device_id_type=MESH)

    def arrived(ref, sem):
        pltpu.make_async_copy(ref, ref, sem).wait()

    own = [
        pltpu.make_async_copy(up, up_t.at[pl.ds(0, 2)], own_sem.at[0]),
        pltpu.make_async_copy(wt, w_t, own_sem.at[1]),
        pltpu.make_async_copy(up, up_s.at[:, tokens(s)], own_sem.at[2]),
        pltpu.make_async_copy(ws, w_s, own_sem.at[3]),
    ]
    for j, (src_t, src_s) in enumerate(((qt, qs), (kt, ks), (vt, vs))):
        own.append(pltpu.make_async_copy(src_t.at[:, :, cols(t)], a_t.at[j, pl.ds(2 * t, 2)], own_sem.at[4 + j]))
        own.append(pltpu.make_async_copy(src_s.at[:, :, cols(s)], a_s.at[j, :, tokens(s)], own_sem.at[7 + j]))
    for copy in own:
        copy.start()
    pl.semaphore_wait(barrier, 9)

    block = part // 2 // PIECES
    quarter = block // n

    def weight_block(p):
        return pl.ds(pl.multiple_of((2 * p + core_id) * block, block), block)

    def weight_quarter(p):
        return pl.ds(pl.multiple_of((2 * p + core_id) * block + x * quarter, quarter), quarter)

    def weights_y(p):
        remote(wt.at[weight_quarter(p)], w_p.at[weight_quarter(p)], wy_sem.at[p], tm=mate).start()

    def weights_x(p):
        ref = w_p.at[weight_quarter(p)]
        arrived(ref, wy_sem.at[p])
        for d in x_others:
            remote(ref, ref, wx_sem.at[p], rep=d).start()

    def weights_c(p):
        arrived(w_p.at[pl.ds(0, 3 * quarter)], wx_sem.at[p])
        ref = w_p.at[weight_block(p)]
        remote(ref, ref, wc_sem.at[p], space=pair).start()

    def weights_here(p):
        arrived(w_p.at[pl.ds(0, block)], wc_sem.at[p])

    def send_space(f):
        for d, slot in ((far, 0), (pair, 1)):
            remote(up.at[f], up_s.at[f, tokens(s)], upz_sem.at[f, slot], space=d).start()
        for j, src in enumerate((qs, ks, vs)):
            for d in (far, cross, pair):
                remote(src.at[f, :, cols(d)], a_s.at[j, f, tokens(s)], qkvz_sem.at[f], space=d).start()

    def pass_space(f):
        arrived(up_s.at[f, pl.ds(0, rows)], upz_sem.at[f, 0])
        remote(up_s.at[f, tokens(far)], up_s.at[f, tokens(far)], upz_sem.at[f, 2], space=pair).start()

    def finish_space(f):
        arrived(up_s.at[f, pl.ds(0, rows)], upz_sem.at[f, 1])
        arrived(up_s.at[f, pl.ds(0, rows)], upz_sem.at[f, 2])
        arrived(a_s.at[:, f, pl.ds(0, 3 * rows)], qkvz_sem.at[f])

    def send_time(i):
        for j, src in enumerate((qt, kt, vt)):
            for d in (y_up, y_down, y_far):
                remote(src.at[:, toks(i), cols(d)], a_t.at[j, pl.ds(2 * t, 2), toks(i)], qkvy_sem.at[i], tm=d).start()

    def time_arrived(i):
        arrived(a_t.at[:, pl.ds(0, 6), toks(i)], qkvy_sem.at[i])

    def project_own():
        og = mul(up_t[...].reshape(4 * rows, width), w_t[...], NT).astype(jnp.bfloat16).reshape(4, rows, part)
        og_t[pl.ds(2 * t, 2)] = og[:2]
        og_t[pl.ds(2 * mirror, 2)] = og[2:]

    def project_mate():
        og_p[...] = mul(up_t[...].reshape(4 * rows, width), w_p[...], NT).astype(jnp.bfloat16).reshape(4, rows, part)
        for i in range(steps):
            for k, d in ((0, t), (2, mirror)):
                remote(og_p.at[pl.ds(k, 2), toks(i)], og_t.at[pl.ds(2 * d, 2), toks(i)], ogy_sem.at[i], tm=mate).start()

    def time_step(i):
        size = 8 * STEP
        mask = (lax.broadcasted_iota(jnp.int32, (size, size), 0) % STEP
                == lax.broadcasted_iota(jnp.int32, (size, size), 1) % STEP)
        for h in range(heads):
            c = slice(h * HEAD, (h + 1) * HEAD)
            q, k, v = (a_t[j, :, toks(i), c].reshape(size, HEAD) for j in range(3))
            o = og_t[:, toks(i), c].reshape(size, HEAD)
            for j, g in enumerate(attention(q, k, v, o, mask)):
                g_t[j, :, toks(i), c] = g.reshape(8, STEP, HEAD)
        for d in (y_far, y_up, y_down):
            remote(g_t.at[:, pl.ds(2 * d, 2), toks(i)], out.at[pl.ds(3, 3), :, toks(i), cols(t)], gy_sem.at[0], tm=d).start()
        pltpu.make_async_copy(g_t.at[:, pl.ds(2 * t, 2), toks(i)], out.at[pl.ds(3, 3), :, toks(i), cols(t)], gy_sem.at[1]).start()

    def space_part(f):
        og_s[...] = mul(up_s[f], w_s[...], NT).astype(jnp.bfloat16)

        def head(h, carry):
            c = pl.ds(pl.multiple_of(h * HEAD, HEAD), HEAD)
            q, k, v = (a_s[j, f, :, c] for j in range(3))
            for j, g in enumerate(attention(q, k, v, og_s[:, c], None)):
                g_s[j, f, :, c] = g
            return carry

        half = heads // 2
        for b in range(2):
            lax.fori_loop(b * half, (b + 1) * half, head, 0)
            here = pl.ds(b * half * HEAD, half * HEAD)
            there = pl.ds(pl.multiple_of(s * part + b * half * HEAD, HEAD), half * HEAD)
            for d in (far, cross, pair):
                remote(g_s.at[:, f, tokens(d), here], out.at[pl.ds(0, 3), f, :, there], gz_sem.at[0], space=d).start()
            pltpu.make_async_copy(g_s.at[:, f, tokens(s), here], out.at[pl.ds(0, 3), f, :, there], gz_sem.at[1]).start()

    for p in range(PIECES):
        weights_y(p)
    remote(up, up_t.at[pl.ds(2, 2)], upy_sem.at[0], tm=mirror).start()
    send_time(0)
    send_space(0)
    send_time(1)
    for copy in own:
        copy.wait()
    for p in range(PIECES):
        weights_x(p)
    send_time(2)
    send_time(3)
    pass_space(0)
    send_space(1)
    for p in range(PIECES):
        weights_c(p)
    send_time(4)
    send_time(5)
    arrived(up_t.at[pl.ds(2, 2)], upy_sem.at[0])
    project_own()
    for p in range(PIECES):
        weights_here(p)
    project_mate()
    finish_space(0)
    space_part(0)

    def step(i, carry):
        time_arrived(i)
        arrived(og_t.at[pl.ds(0, 4), toks(i)], ogy_sem.at[i])
        time_step(i)

        @pl.when(i == SPATIAL_AFTER)
        def _():
            pass_space(1)
            finish_space(1)
            space_part(1)
        return carry

    lax.fori_loop(0, steps, step, 0)

    arrived(out.at[pl.ds(0, 3), :, :, pl.ds(0, part)], gz_sem.at[1])
    arrived(out.at[pl.ds(0, 3), :, :, pl.ds(0, 3 * part)], gz_sem.at[0])
    arrived(out.at[pl.ds(3, 3), :, :, pl.ds(0, part)], gy_sem.at[1])
    arrived(out.at[pl.ds(3, 3), :, :, pl.ds(0, 3 * part)], gy_sem.at[0])
    arrived(w_p, send_sem.at[0])
    for _ in range(4):
        arrived(up_t.at[pl.ds(0, 2)], send_sem.at[0])
    arrived(og_p, send_sem.at[0])
    for ref in (a_s.at[:, :, pl.ds(0, 3 * rows)], a_t.at[:, pl.ds(0, 6)]):
        arrived(ref, send_sem.at[0])
        arrived(ref, send_sem.at[0])


def local(*args):
    up, ws = args[6], args[7]
    frames, rows, width = up.shape
    part = ws.shape[0]
    bf = jnp.bfloat16
    anywhere = pl.BlockSpec(memory_space=pl.ANY)
    whole = pl.pallas_call(
        core,
        out_shape=pltpu.VMEM((6, frames, rows, width), bf),
        in_specs=[pl.BlockSpec(memory_space=pltpu.HBM)] * 9,
        out_specs=pl.BlockSpec(memory_space=pltpu.VMEM),
        scratch_shapes=[
            pltpu.VMEM((frames, 4 * rows, width), bf),
            pltpu.VMEM((2 * frames, rows, width), bf),
            pltpu.VMEM((3, frames, 4 * rows, part), bf),
            pltpu.VMEM((3, 4 * frames, rows, part), bf),
            pltpu.VMEM((part, width), bf),
            pltpu.VMEM((part, width), bf),
            pltpu.VMEM((part, width), bf),
            pltpu.VMEM((4 * rows, part), bf),
            pltpu.VMEM((4 * frames, rows, part), bf),
            pltpu.VMEM((2 * frames, rows, part), bf),
            pltpu.VMEM((3, frames, 4 * rows, part), bf),
            pltpu.VMEM((3, 4 * frames, rows, part), bf),
            pltpu.SemaphoreType.DMA((10,)),
            pltpu.SemaphoreType.DMA((frames, 3)),
            pltpu.SemaphoreType.DMA((frames,)),
            pltpu.SemaphoreType.DMA((1,)),
            pltpu.SemaphoreType.DMA((rows // STEP,)),
            pltpu.SemaphoreType.DMA((rows // STEP,)),
            pltpu.SemaphoreType.DMA((PIECES,)),
            pltpu.SemaphoreType.DMA((PIECES,)),
            pltpu.SemaphoreType.DMA((PIECES,)),
            pltpu.SemaphoreType.DMA((2,)),
            pltpu.SemaphoreType.DMA((2,)),
            pltpu.SemaphoreType.DMA((1,)),
        ],
        compiler_params=pltpu.CompilerParams(
            collective_id=0, has_side_effects=True, vmem_limit_bytes=57 * 1024 * 1024),
        name="core",
    )(*args)
    return tuple(whole[j] for j in range(6))


def solution(mesh):
    rows = P(("rep", "tm"), "space", None)
    in_specs = (rows,) * 7 + (P("space", None), P("tm", None))
    return jax.shard_map(local, mesh=mesh, in_specs=in_specs, out_specs=(rows,) * 6, check_vma=False)
```

```python
import jax
import jax.numpy as jnp
from jax import lax
from jax.experimental import pallas as pl
from jax.experimental.pallas import tpu as pltpu
from jax.sharding import PartitionSpec as P

HEAD = 128
SCALE = HEAD ** (-0.5)
MESH = pl.DeviceIdType.MESH
STEP = 16
SPATIAL_AFTER = 1
PIECES = 2
NT = (((1,), (1,)), ((), ()))
NN = (((1,), (0,)), ((), ()))
TN = (((0,), (0,)), ((), ()))


def mul(a, b, dims):
    return lax.dot_general(a, b, dims, preferred_element_type=jnp.float32)


def attention(q, k, v, o, mask):
    scores = mul(k, q, NT) * SCALE
    if mask is not None:
        scores = jnp.where(mask, scores, -3.0e38)
    e = jnp.exp(scores - jnp.max(scores, axis=0, keepdims=True))
    a = e * (1.0 / jnp.sum(e, axis=0, keepdims=True))
    gv = mul(a.astype(jnp.bfloat16), o, NN)
    da = mul(v, o, NT)
    ds = a * (da - jnp.sum(a * da, axis=0, keepdims=True))
    low = (ds * SCALE).astype(jnp.bfloat16)
    gk = mul(low, q, NN)
    gq = mul(low, k, TN)
    return gq.astype(jnp.bfloat16), gk.astype(jnp.bfloat16), gv.astype(jnp.bfloat16)


def core(qs, ks, vs, qt, kt, vt, up, ws, wt, out,
         up_s, up_t, a_s, a_t, w_s, w_t, w_p, og_s, og_t, og_p, g_s, g_t,
         own_sem, upz_sem, qkvz_sem, upy_sem, qkvy_sem, ogy_sem, wy_sem, wx_sem, wc_sem, gz_sem, gy_sem, send_sem, ready_y, ready_z, ready_x):
    frames, rows, width = up.shape
    part = a_s.shape[-1]
    heads = part // HEAD
    steps = rows // STEP
    r = lax.axis_index("rep")
    t = lax.axis_index("tm")
    s = lax.axis_index("space")
    n = 4
    x = r // 2
    core_id = lax.rem(s, 2)
    y_up, y_down, y_far = lax.rem(t + 1, n), lax.rem(t + n - 1, n), lax.rem(t + 2, n)
    mate = t + 1 - 2 * lax.rem(t, 2)
    mirror = n - 1 - t
    pair = s + 1 - 2 * core_id
    far = lax.rem(s + 2, n)
    cross = lax.rem(pair + 2, n)
    x_others = [lax.rem(x + k, n) * 2 + lax.rem(r, 2) for k in (1, 3, 2)]

    barrier = pltpu.get_barrier_semaphore()
    half_z = s // 2
    y_others = (y_up, y_down, y_far)
    x_index = [lax.rem(x + k, n) for k in (1, 3, 2)]

    def signal_if(condition, semaphore, **where):
        @pl.when(condition)
        def _():
            pl.semaphore_signal(semaphore, inc=1, device_id=where, device_id_type=MESH)

    pl.semaphore_signal(barrier, inc=1, device_id={"space": pair}, device_id_type=MESH)
    for d in y_others:
        signal_if(d > t, barrier, tm=d)
    for d in (far, cross):
        signal_if(half_z == 0, barrier, space=d)
    for k, d in zip(x_index, x_others):
        signal_if(k > x, barrier, rep=d)

    def cols(d):
        return pl.ds(pl.multiple_of(d * part, part), part)

    def tokens(d):
        return pl.ds(pl.multiple_of(d * rows, rows), rows)

    def toks(i):
        return pl.ds(pl.multiple_of(i * STEP, STEP), STEP)

    def remote(src, dst, sem, **where):
        return pltpu.make_async_remote_copy(
            src, dst, send_sem.at[0], sem, device_id=where, device_id_type=MESH)

    def arrived(ref, sem):
        pltpu.make_async_copy(ref, ref, sem).wait()

    own = [
        pltpu.make_async_copy(up, up_t.at[pl.ds(0, 2)], own_sem.at[0]),
        pltpu.make_async_copy(wt, w_t, own_sem.at[1]),
        pltpu.make_async_copy(up, up_s.at[:, tokens(s)], own_sem.at[2]),
        pltpu.make_async_copy(ws, w_s, own_sem.at[3]),
    ]
    for j, (src_t, src_s) in enumerate(((qt, qs), (kt, ks), (vt, vs))):
        own.append(pltpu.make_async_copy(src_t.at[:, :, cols(t)], a_t.at[j, pl.ds(2 * t, 2)], own_sem.at[4 + j]))
        own.append(pltpu.make_async_copy(src_s.at[:, :, cols(s)], a_s.at[j, :, tokens(s)], own_sem.at[7 + j]))
    for copy in own:
        copy.start()
    pl.semaphore_wait(barrier, 1 + t + 2 * half_z + x)
    for d in y_others:
        signal_if(d < t, ready_y, tm=d)
    for d in (far, cross):
        signal_if(half_z == 1, ready_z, space=d)
    for k, d in zip(x_index, x_others):
        signal_if(k < x, ready_x, rep=d)

    block = part // 2 // PIECES
    quarter = block // n

    def weight_block(p):
        return pl.ds(pl.multiple_of((2 * p + core_id) * block, block), block)

    def weight_quarter(p):
        return pl.ds(pl.multiple_of((2 * p + core_id) * block + x * quarter, quarter), quarter)

    def weights_y(p):
        remote(wt.at[weight_quarter(p)], w_p.at[weight_quarter(p)], wy_sem.at[p], tm=mate).start()

    def weights_x(p):
        ref = w_p.at[weight_quarter(p)]
        arrived(ref, wy_sem.at[p])
        for d in x_others:
            remote(ref, ref, wx_sem.at[p], rep=d).start()

    def weights_c(p):
        arrived(w_p.at[pl.ds(0, 3 * quarter)], wx_sem.at[p])
        ref = w_p.at[weight_block(p)]
        remote(ref, ref, wc_sem.at[p], space=pair).start()

    def weights_here(p):
        arrived(w_p.at[pl.ds(0, block)], wc_sem.at[p])

    def send_space(f):
        for d, slot in ((far, 0), (pair, 1)):
            remote(up.at[f], up_s.at[f, tokens(s)], upz_sem.at[f, slot], space=d).start()
        for j, src in enumerate((qs, ks, vs)):
            for d in (far, cross, pair):
                remote(src.at[f, :, cols(d)], a_s.at[j, f, tokens(s)], qkvz_sem.at[f], space=d).start()

    def pass_space(f):
        arrived(up_s.at[f, pl.ds(0, rows)], upz_sem.at[f, 0])
        remote(up_s.at[f, tokens(far)], up_s.at[f, tokens(far)], upz_sem.at[f, 2], space=pair).start()

    def finish_space(f):
        arrived(up_s.at[f, pl.ds(0, rows)], upz_sem.at[f, 1])
        arrived(up_s.at[f, pl.ds(0, rows)], upz_sem.at[f, 2])
        arrived(a_s.at[:, f, pl.ds(0, 3 * rows)], qkvz_sem.at[f])

    def send_time(i):
        for j, src in enumerate((qt, kt, vt)):
            for d in (y_up, y_down, y_far):
                remote(src.at[:, toks(i), cols(d)], a_t.at[j, pl.ds(2 * t, 2), toks(i)], qkvy_sem.at[i], tm=d).start()

    def time_arrived(i):
        arrived(a_t.at[:, pl.ds(0, 6), toks(i)], qkvy_sem.at[i])

    def project_own():
        og = mul(up_t[...].reshape(4 * rows, width), w_t[...], NT).astype(jnp.bfloat16).reshape(4, rows, part)
        og_t[pl.ds(2 * t, 2)] = og[:2]
        og_t[pl.ds(2 * mirror, 2)] = og[2:]

    def project_mate():
        og_p[...] = mul(up_t[...].reshape(4 * rows, width), w_p[...], NT).astype(jnp.bfloat16).reshape(4, rows, part)
        for i in range(steps):
            for k, d in ((0, t), (2, mirror)):
                remote(og_p.at[pl.ds(k, 2), toks(i)], og_t.at[pl.ds(2 * d, 2), toks(i)], ogy_sem.at[i], tm=mate).start()

    def time_step(i):
        size = 8 * STEP
        mask = (lax.broadcasted_iota(jnp.int32, (size, size), 0) % STEP
                == lax.broadcasted_iota(jnp.int32, (size, size), 1) % STEP)
        for h in range(heads):
            c = slice(h * HEAD, (h + 1) * HEAD)
            q, k, v = (a_t[j, :, toks(i), c].reshape(size, HEAD) for j in range(3))
            o = og_t[:, toks(i), c].reshape(size, HEAD)
            for j, g in enumerate(attention(q, k, v, o, mask)):
                g_t[j, :, toks(i), c] = g.reshape(8, STEP, HEAD)
        for d in (y_far, y_up, y_down):
            remote(g_t.at[:, pl.ds(2 * d, 2), toks(i)], out.at[pl.ds(3, 3), :, toks(i), cols(t)], gy_sem.at[0], tm=d).start()
        pltpu.make_async_copy(g_t.at[:, pl.ds(2 * t, 2), toks(i)], out.at[pl.ds(3, 3), :, toks(i), cols(t)], gy_sem.at[1]).start()

    def space_part(f):
        og_s[...] = mul(up_s[f], w_s[...], NT).astype(jnp.bfloat16)

        def head(h, carry):
            c = pl.ds(pl.multiple_of(h * HEAD, HEAD), HEAD)
            q, k, v = (a_s[j, f, :, c] for j in range(3))
            for j, g in enumerate(attention(q, k, v, og_s[:, c], None)):
                g_s[j, f, :, c] = g
            return carry

        half = heads // 2
        for b in range(2):
            lax.fori_loop(b * half, (b + 1) * half, head, 0)
            here = pl.ds(b * half * HEAD, half * HEAD)
            there = pl.ds(pl.multiple_of(s * part + b * half * HEAD, HEAD), half * HEAD)
            for d in (far, cross, pair):
                remote(g_s.at[:, f, tokens(d), here], out.at[pl.ds(0, 3), f, :, there], gz_sem.at[0], space=d).start()
            pltpu.make_async_copy(g_s.at[:, f, tokens(s), here], out.at[pl.ds(0, 3), f, :, there], gz_sem.at[1]).start()

    @pl.when(half_z == 1)
    def _():
        send_space(0)

    @pl.when(t < n - 1)
    def _():
        pl.semaphore_wait(ready_y, n - 1 - t)

    for p in range(PIECES):
        weights_y(p)
    remote(up, up_t.at[pl.ds(2, 2)], upy_sem.at[0], tm=mirror).start()
    send_time(0)
    send_time(1)

    @pl.when(half_z == 0)
    def _():
        pl.semaphore_wait(ready_z, 2)
        send_space(0)

    @pl.when(x < n - 1)
    def _():
        pl.semaphore_wait(ready_x, n - 1 - x)

    for copy in own:
        copy.wait()
    for p in range(PIECES):
        weights_x(p)
    send_time(2)
    send_time(3)
    pass_space(0)
    send_space(1)
    for p in range(PIECES):
        weights_c(p)
    send_time(4)
    send_time(5)
    arrived(up_t.at[pl.ds(2, 2)], upy_sem.at[0])
    project_own()
    for p in range(PIECES):
        weights_here(p)
    project_mate()
    finish_space(0)
    space_part(0)

    def step(i, carry):
        time_arrived(i)
        arrived(og_t.at[pl.ds(0, 4), toks(i)], ogy_sem.at[i])
        time_step(i)

        @pl.when(i == SPATIAL_AFTER)
        def _():
            pass_space(1)
            finish_space(1)
            space_part(1)
        return carry

    lax.fori_loop(0, steps, step, 0)

    arrived(out.at[pl.ds(0, 3), :, :, pl.ds(0, part)], gz_sem.at[1])
    arrived(out.at[pl.ds(0, 3), :, :, pl.ds(0, 3 * part)], gz_sem.at[0])
    arrived(out.at[pl.ds(3, 3), :, :, pl.ds(0, part)], gy_sem.at[1])
    arrived(out.at[pl.ds(3, 3), :, :, pl.ds(0, 3 * part)], gy_sem.at[0])
    arrived(w_p, send_sem.at[0])
    for _ in range(4):
        arrived(up_t.at[pl.ds(0, 2)], send_sem.at[0])
    arrived(og_p, send_sem.at[0])
    for ref in (a_s.at[:, :, pl.ds(0, 3 * rows)], a_t.at[:, pl.ds(0, 6)]):
        arrived(ref, send_sem.at[0])
        arrived(ref, send_sem.at[0])


def local(*args):
    up, ws = args[6], args[7]
    frames, rows, width = up.shape
    part = ws.shape[0]
    bf = jnp.bfloat16
    anywhere = pl.BlockSpec(memory_space=pl.ANY)
    whole = pl.pallas_call(
        core,
        out_shape=pltpu.VMEM((6, frames, rows, width), bf),
        in_specs=[pl.BlockSpec(memory_space=pltpu.HBM)] * 9,
        out_specs=pl.BlockSpec(memory_space=pltpu.VMEM),
        scratch_shapes=[
            pltpu.VMEM((frames, 4 * rows, width), bf),
            pltpu.VMEM((2 * frames, rows, width), bf),
            pltpu.VMEM((3, frames, 4 * rows, part), bf),
            pltpu.VMEM((3, 4 * frames, rows, part), bf),
            pltpu.VMEM((part, width), bf),
            pltpu.VMEM((part, width), bf),
            pltpu.VMEM((part, width), bf),
            pltpu.VMEM((4 * rows, part), bf),
            pltpu.VMEM((4 * frames, rows, part), bf),
            pltpu.VMEM((2 * frames, rows, part), bf),
            pltpu.VMEM((3, frames, 4 * rows, part), bf),
            pltpu.VMEM((3, 4 * frames, rows, part), bf),
            pltpu.SemaphoreType.DMA((10,)),
            pltpu.SemaphoreType.DMA((frames, 3)),
            pltpu.SemaphoreType.DMA((frames,)),
            pltpu.SemaphoreType.DMA((1,)),
            pltpu.SemaphoreType.DMA((rows // STEP,)),
            pltpu.SemaphoreType.DMA((rows // STEP,)),
            pltpu.SemaphoreType.DMA((PIECES,)),
            pltpu.SemaphoreType.DMA((PIECES,)),
            pltpu.SemaphoreType.DMA((PIECES,)),
            pltpu.SemaphoreType.DMA((2,)),
            pltpu.SemaphoreType.DMA((2,)),
            pltpu.SemaphoreType.DMA((1,)),
            pltpu.SemaphoreType.REGULAR,
            pltpu.SemaphoreType.REGULAR,
            pltpu.SemaphoreType.REGULAR,
        ],
        compiler_params=pltpu.CompilerParams(
            collective_id=0, has_side_effects=True, vmem_limit_bytes=57 * 1024 * 1024),
        name="core",
    )(*args)
    return tuple(whole[j] for j in range(6))


def solution(mesh):
    rows = P(("rep", "tm"), "space", None)
    in_specs = (rows,) * 7 + (P("space", None), P("tm", None))
    return jax.shard_map(local, mesh=mesh, in_specs=in_specs, out_specs=(rows,) * 6, check_vma=False)
```

```python
import jax
import jax.numpy as jnp
from jax import lax
from jax.experimental import pallas as pl
from jax.experimental.pallas import tpu as pltpu
from jax.sharding import PartitionSpec as P

HEAD = 128
SCALE = HEAD ** (-0.5)
MESH = pl.DeviceIdType.MESH
STEP = 16
SPATIAL_AFTER = 2
PIECES = 2
NT = (((1,), (1,)), ((), ()))
NN = (((1,), (0,)), ((), ()))
TN = (((0,), (0,)), ((), ()))


def mul(a, b, dims):
    return lax.dot_general(a, b, dims, preferred_element_type=jnp.float32)


def attention(q, k, v, o, mask):
    scores = mul(k, q, NT) * SCALE
    if mask is not None:
        scores = jnp.where(mask, scores, -3.0e38)
    e = jnp.exp(scores - jnp.max(scores, axis=0, keepdims=True))
    a = e * (1.0 / jnp.sum(e, axis=0, keepdims=True))
    gv = mul(a.astype(jnp.bfloat16), o, NN)
    da = mul(v, o, NT)
    ds = a * (da - jnp.sum(a * da, axis=0, keepdims=True))
    low = (ds * SCALE).astype(jnp.bfloat16)
    gk = mul(low, q, NN)
    gq = mul(low, k, TN)
    return gq.astype(jnp.bfloat16), gk.astype(jnp.bfloat16), gv.astype(jnp.bfloat16)


def core(qs, ks, vs, qt, kt, vt, up, ws, wt, out,
         up_s, up_t, a_s, a_t, w_s, w_t, w_p, og_s, og_t, og_p, g_s, g_t,
         own_sem, upz_sem, qkvz_sem, upy_sem, qkvy_sem, ogy_sem, wy_sem, wx_sem, wc_sem, gz_sem, gy_sem, send_sem, ready_y, ready_z, ready_x):
    frames, rows, width = up.shape
    part = a_s.shape[-1]
    heads = part // HEAD
    steps = rows // STEP
    r = lax.axis_index("rep")
    t = lax.axis_index("tm")
    s = lax.axis_index("space")
    n = 4
    x = r // 2
    core_id = lax.rem(s, 2)
    y_up, y_down, y_far = lax.rem(t + 1, n), lax.rem(t + n - 1, n), lax.rem(t + 2, n)
    mate = t + 1 - 2 * lax.rem(t, 2)
    mirror = n - 1 - t
    pair = s + 1 - 2 * core_id
    far = lax.rem(s + 2, n)
    cross = lax.rem(pair + 2, n)
    x_others = [lax.rem(x + k, n) * 2 + lax.rem(r, 2) for k in (1, 3, 2)]

    barrier = pltpu.get_barrier_semaphore()
    half_z = s // 2
    y_others = (y_up, y_down, y_far)
    x_index = [lax.rem(x + k, n) for k in (1, 3, 2)]

    def signal_if(condition, semaphore, **where):
        @pl.when(condition)
        def _():
            pl.semaphore_signal(semaphore, inc=1, device_id=where, device_id_type=MESH)

    pl.semaphore_signal(barrier, inc=1, device_id={"space": pair}, device_id_type=MESH)
    for d in y_others:
        signal_if(d > t, barrier, tm=d)
    for d in (far, cross):
        signal_if(half_z == 0, barrier, space=d)
    for k, d in zip(x_index, x_others):
        signal_if(k > x, barrier, rep=d)

    def cols(d):
        return pl.ds(pl.multiple_of(d * part, part), part)

    def tokens(d):
        return pl.ds(pl.multiple_of(d * rows, rows), rows)

    def toks(i):
        return pl.ds(pl.multiple_of(i * STEP, STEP), STEP)

    def remote(src, dst, sem, **where):
        return pltpu.make_async_remote_copy(
            src, dst, send_sem.at[0], sem, device_id=where, device_id_type=MESH)

    def arrived(ref, sem):
        pltpu.make_async_copy(ref, ref, sem).wait()

    own = [
        pltpu.make_async_copy(up, up_t.at[pl.ds(0, 2)], own_sem.at[0]),
        pltpu.make_async_copy(wt, w_t, own_sem.at[1]),
        pltpu.make_async_copy(up, up_s.at[:, tokens(s)], own_sem.at[2]),
        pltpu.make_async_copy(ws, w_s, own_sem.at[3]),
    ]
    for j, (src_t, src_s) in enumerate(((qt, qs), (kt, ks), (vt, vs))):
        own.append(pltpu.make_async_copy(src_t.at[:, :, cols(t)], a_t.at[j, pl.ds(2 * t, 2)], own_sem.at[4 + j]))
        own.append(pltpu.make_async_copy(src_s.at[:, :, cols(s)], a_s.at[j, :, tokens(s)], own_sem.at[7 + j]))
    for copy in own:
        copy.start()
    pl.semaphore_wait(barrier, 1 + t + 2 * half_z + x)
    for d in y_others:
        signal_if(d < t, ready_y, tm=d)
    for d in (far, cross):
        signal_if(half_z == 1, ready_z, space=d)
    for k, d in zip(x_index, x_others):
        signal_if(k < x, ready_x, rep=d)

    block = part // 2 // PIECES
    quarter = block // n

    def weight_block(p):
        return pl.ds(pl.multiple_of((2 * p + core_id) * block, block), block)

    def weight_quarter(p):
        return pl.ds(pl.multiple_of((2 * p + core_id) * block + x * quarter, quarter), quarter)

    def weights_y(p):
        remote(wt.at[weight_quarter(p)], w_p.at[weight_quarter(p)], wy_sem.at[p], tm=mate).start()

    def weights_x(p):
        ref = w_p.at[weight_quarter(p)]
        arrived(ref, wy_sem.at[p])
        for d in x_others:
            remote(ref, ref, wx_sem.at[p], rep=d).start()

    def weights_c(p):
        arrived(w_p.at[pl.ds(0, 3 * quarter)], wx_sem.at[p])
        ref = w_p.at[weight_block(p)]
        remote(ref, ref, wc_sem.at[p], space=pair).start()

    def weights_here(p):
        arrived(w_p.at[pl.ds(0, block)], wc_sem.at[p])

    def send_space(f):
        for d, slot in ((far, 0), (pair, 1)):
            remote(up.at[f], up_s.at[f, tokens(s)], upz_sem.at[f, slot], space=d).start()
        for j, src in enumerate((qs, ks, vs)):
            for d in (far, cross, pair):
                remote(src.at[f, :, cols(d)], a_s.at[j, f, tokens(s)], qkvz_sem.at[f], space=d).start()

    def pass_space(f):
        arrived(up_s.at[f, pl.ds(0, rows)], upz_sem.at[f, 0])
        remote(up_s.at[f, tokens(far)], up_s.at[f, tokens(far)], upz_sem.at[f, 2], space=pair).start()

    def finish_space(f):
        arrived(up_s.at[f, pl.ds(0, rows)], upz_sem.at[f, 1])
        arrived(up_s.at[f, pl.ds(0, rows)], upz_sem.at[f, 2])
        arrived(a_s.at[:, f, pl.ds(0, 3 * rows)], qkvz_sem.at[f])

    def send_time(i):
        for j, src in enumerate((qt, kt, vt)):
            for d in (y_up, y_down, y_far):
                remote(src.at[:, toks(i), cols(d)], a_t.at[j, pl.ds(2 * t, 2), toks(i)], qkvy_sem.at[i], tm=d).start()

    def time_arrived(i):
        arrived(a_t.at[:, pl.ds(0, 6), toks(i)], qkvy_sem.at[i])

    def project_own():
        og = mul(up_t[...].reshape(4 * rows, width), w_t[...], NT).astype(jnp.bfloat16).reshape(4, rows, part)
        og_t[pl.ds(2 * t, 2)] = og[:2]
        og_t[pl.ds(2 * mirror, 2)] = og[2:]

    def project_mate():
        og_p[...] = mul(up_t[...].reshape(4 * rows, width), w_p[...], NT).astype(jnp.bfloat16).reshape(4, rows, part)
        for i in range(steps):
            for k, d in ((0, t), (2, mirror)):
                remote(og_p.at[pl.ds(k, 2), toks(i)], og_t.at[pl.ds(2 * d, 2), toks(i)], ogy_sem.at[i], tm=mate).start()

    def time_step(i):
        size = 8 * STEP
        mask = (lax.broadcasted_iota(jnp.int32, (size, size), 0) % STEP
                == lax.broadcasted_iota(jnp.int32, (size, size), 1) % STEP)
        for h in range(heads):
            c = slice(h * HEAD, (h + 1) * HEAD)
            q, k, v = (a_t[j, :, toks(i), c].reshape(size, HEAD) for j in range(3))
            o = og_t[:, toks(i), c].reshape(size, HEAD)
            for j, g in enumerate(attention(q, k, v, o, mask)):
                g_t[j, :, toks(i), c] = g.reshape(8, STEP, HEAD)
        for d in (y_far, y_up, y_down):
            remote(g_t.at[:, pl.ds(2 * d, 2), toks(i)], out.at[pl.ds(3, 3), :, toks(i), cols(t)], gy_sem.at[0], tm=d).start()
        pltpu.make_async_copy(g_t.at[:, pl.ds(2 * t, 2), toks(i)], out.at[pl.ds(3, 3), :, toks(i), cols(t)], gy_sem.at[1]).start()

    def space_part(f):
        og_s[...] = mul(up_s[f], w_s[...], NT).astype(jnp.bfloat16)

        def head(h, carry):
            c = pl.ds(pl.multiple_of(h * HEAD, HEAD), HEAD)
            q, k, v = (a_s[j, f, :, c] for j in range(3))
            for j, g in enumerate(attention(q, k, v, og_s[:, c], None)):
                g_s[j, f, :, c] = g
            return carry

        half = heads // 2
        for b in range(2):
            lax.fori_loop(b * half, (b + 1) * half, head, 0)
            here = pl.ds(b * half * HEAD, half * HEAD)
            there = pl.ds(pl.multiple_of(s * part + b * half * HEAD, HEAD), half * HEAD)
            for d in (far, cross, pair):
                remote(g_s.at[:, f, tokens(d), here], out.at[pl.ds(0, 3), f, :, there], gz_sem.at[0], space=d).start()
            pltpu.make_async_copy(g_s.at[:, f, tokens(s), here], out.at[pl.ds(0, 3), f, :, there], gz_sem.at[1]).start()

    @pl.when(half_z == 1)
    def _():
        send_space(0)

    @pl.when(t < n - 1)
    def _():
        pl.semaphore_wait(ready_y, n - 1 - t)

    for p in range(PIECES):
        weights_y(p)
    remote(up, up_t.at[pl.ds(2, 2)], upy_sem.at[0], tm=mirror).start()
    send_time(0)
    send_time(1)

    @pl.when(half_z == 0)
    def _():
        pl.semaphore_wait(ready_z, 2)
        send_space(0)

    @pl.when(x < n - 1)
    def _():
        pl.semaphore_wait(ready_x, n - 1 - x)

    for copy in own:
        copy.wait()
    for p in range(PIECES):
        weights_x(p)
    send_time(2)
    send_time(3)
    pass_space(0)
    send_space(1)
    for p in range(PIECES):
        weights_c(p)
    send_time(4)
    send_time(5)
    arrived(up_t.at[pl.ds(2, 2)], upy_sem.at[0])
    project_own()
    for p in range(PIECES):
        weights_here(p)
    project_mate()
    finish_space(0)
    space_part(0)

    def step(i, carry):
        time_arrived(i)
        arrived(og_t.at[pl.ds(0, 4), toks(i)], ogy_sem.at[i])
        time_step(i)

        @pl.when(i == SPATIAL_AFTER)
        def _():
            pass_space(1)
            finish_space(1)
            space_part(1)
        return carry

    lax.fori_loop(0, steps, step, 0)

    arrived(out.at[pl.ds(0, 3), :, :, pl.ds(0, part)], gz_sem.at[1])
    arrived(out.at[pl.ds(0, 3), :, :, pl.ds(0, 3 * part)], gz_sem.at[0])
    arrived(out.at[pl.ds(3, 3), :, :, pl.ds(0, part)], gy_sem.at[1])
    arrived(out.at[pl.ds(3, 3), :, :, pl.ds(0, 3 * part)], gy_sem.at[0])
    arrived(w_p, send_sem.at[0])
    for _ in range(4):
        arrived(up_t.at[pl.ds(0, 2)], send_sem.at[0])
    arrived(og_p, send_sem.at[0])
    for ref in (a_s.at[:, :, pl.ds(0, 3 * rows)], a_t.at[:, pl.ds(0, 6)]):
        arrived(ref, send_sem.at[0])
        arrived(ref, send_sem.at[0])


def local(*args):
    up, ws = args[6], args[7]
    frames, rows, width = up.shape
    part = ws.shape[0]
    bf = jnp.bfloat16
    anywhere = pl.BlockSpec(memory_space=pl.ANY)
    whole = pl.pallas_call(
        core,
        out_shape=pltpu.VMEM((6, frames, rows, width), bf),
        in_specs=[pl.BlockSpec(memory_space=pltpu.HBM)] * 9,
        out_specs=pl.BlockSpec(memory_space=pltpu.VMEM),
        scratch_shapes=[
            pltpu.VMEM((frames, 4 * rows, width), bf),
            pltpu.VMEM((2 * frames, rows, width), bf),
            pltpu.VMEM((3, frames, 4 * rows, part), bf),
            pltpu.VMEM((3, 4 * frames, rows, part), bf),
            pltpu.VMEM((part, width), bf),
            pltpu.VMEM((part, width), bf),
            pltpu.VMEM((part, width), bf),
            pltpu.VMEM((4 * rows, part), bf),
            pltpu.VMEM((4 * frames, rows, part), bf),
            pltpu.VMEM((2 * frames, rows, part), bf),
            pltpu.VMEM((3, frames, 4 * rows, part), bf),
            pltpu.VMEM((3, 4 * frames, rows, part), bf),
            pltpu.SemaphoreType.DMA((10,)),
            pltpu.SemaphoreType.DMA((frames, 3)),
            pltpu.SemaphoreType.DMA((frames,)),
            pltpu.SemaphoreType.DMA((1,)),
            pltpu.SemaphoreType.DMA((rows // STEP,)),
            pltpu.SemaphoreType.DMA((rows // STEP,)),
            pltpu.SemaphoreType.DMA((PIECES,)),
            pltpu.SemaphoreType.DMA((PIECES,)),
            pltpu.SemaphoreType.DMA((PIECES,)),
            pltpu.SemaphoreType.DMA((2,)),
            pltpu.SemaphoreType.DMA((2,)),
            pltpu.SemaphoreType.DMA((1,)),
            pltpu.SemaphoreType.REGULAR,
            pltpu.SemaphoreType.REGULAR,
            pltpu.SemaphoreType.REGULAR,
        ],
        compiler_params=pltpu.CompilerParams(
            collective_id=0, has_side_effects=True, vmem_limit_bytes=57 * 1024 * 1024),
        name="core",
    )(*args)
    return tuple(whole[j] for j in range(6))


def solution(mesh):
    rows = P(("rep", "tm"), "space", None)
    in_specs = (rows,) * 7 + (P("space", None), P("tm", None))
    return jax.shard_map(local, mesh=mesh, in_specs=in_specs, out_specs=(rows,) * 6, check_vma=False)
```

```python
import jax
import jax.numpy as jnp
from jax import lax
from jax.experimental import pallas as pl
from jax.experimental.pallas import tpu as pltpu
from jax.sharding import PartitionSpec as P

HEAD = 128
SCALE = HEAD ** (-0.5)
MESH = pl.DeviceIdType.MESH
STEP = 16
SPATIAL_AFTER = 2
PIECES = 2
NT = (((1,), (1,)), ((), ()))
NN = (((1,), (0,)), ((), ()))
TN = (((0,), (0,)), ((), ()))


def mul(a, b, dims):
    return lax.dot_general(a, b, dims, preferred_element_type=jnp.float32)


def attention(q, k, v, o, mask):
    scores = mul(k, q, NT) * SCALE
    if mask is not None:
        scores = jnp.where(mask, scores, -3.0e38)
    e = jnp.exp(scores - jnp.max(scores, axis=0, keepdims=True))
    a = e * (1.0 / jnp.sum(e, axis=0, keepdims=True))
    gv = mul(a.astype(jnp.bfloat16), o, NN)
    da = mul(v, o, NT)
    ds = a * (da - jnp.sum(a * da, axis=0, keepdims=True))
    low = (ds * SCALE).astype(jnp.bfloat16)
    gk = mul(low, q, NN)
    gq = mul(low, k, TN)
    return gq.astype(jnp.bfloat16), gk.astype(jnp.bfloat16), gv.astype(jnp.bfloat16)


def core(qs, ks, vs, qt, kt, vt, up, ws, wt, out,
         up_s, up_t, a_s, a_t, w_s, w_t, w_p, og_s, og_t, og_p, g_s, g_t,
         own_sem, upz_sem, qkvz_sem, upy_sem, qkvy_sem, ogy_sem, wy_sem, wx_sem, wc_sem, gz_sem, gy_sem, send_sem, ready_y, ready_z, ready_x):
    frames, rows, width = up.shape
    part = a_s.shape[-1]
    heads = part // HEAD
    steps = rows // STEP
    r = lax.axis_index("rep")
    t = lax.axis_index("tm")
    s = lax.axis_index("space")
    n = 4
    x = r // 2
    core_id = lax.rem(s, 2)
    y_up, y_down, y_far = lax.rem(t + 1, n), lax.rem(t + n - 1, n), lax.rem(t + 2, n)
    mate = t + 1 - 2 * lax.rem(t, 2)
    mirror = n - 1 - t
    pair = s + 1 - 2 * core_id
    far = lax.rem(s + 2, n)
    cross = lax.rem(pair + 2, n)
    x_others = [lax.rem(x + k, n) * 2 + lax.rem(r, 2) for k in (1, 3, 2)]

    barrier = pltpu.get_barrier_semaphore()
    half_z = s // 2
    y_others = (y_up, y_down, y_far)
    x_index = [lax.rem(x + k, n) for k in (1, 3, 2)]

    def signal_if(condition, semaphore, **where):
        @pl.when(condition)
        def _():
            pl.semaphore_signal(semaphore, inc=1, device_id=where, device_id_type=MESH)

    pl.semaphore_signal(barrier, inc=1, device_id={"space": pair}, device_id_type=MESH)
    for d in y_others:
        signal_if(d > t, barrier, tm=d)
    for d in (far, cross):
        signal_if(half_z == 0, barrier, space=d)
    for k, d in zip(x_index, x_others):
        signal_if(k > x, barrier, rep=d)

    def cols(d):
        return pl.ds(pl.multiple_of(d * part, part), part)

    def tokens(d):
        return pl.ds(pl.multiple_of(d * rows, rows), rows)

    def toks(i):
        return pl.ds(pl.multiple_of(i * STEP, STEP), STEP)

    def remote(src, dst, sem, **where):
        return pltpu.make_async_remote_copy(
            src, dst, send_sem.at[0], sem, device_id=where, device_id_type=MESH)

    def arrived(ref, sem):
        pltpu.make_async_copy(ref, ref, sem).wait()

    own = [
        pltpu.make_async_copy(up, up_t.at[pl.ds(0, 2)], own_sem.at[0]),
        pltpu.make_async_copy(wt, w_t, own_sem.at[1]),
        pltpu.make_async_copy(up, up_s.at[:, tokens(s)], own_sem.at[2]),
        pltpu.make_async_copy(ws, w_s, own_sem.at[3]),
    ]
    for j, (src_t, src_s) in enumerate(((qt, qs), (kt, ks), (vt, vs))):
        own.append(pltpu.make_async_copy(src_t.at[:, :, cols(t)], a_t.at[j, pl.ds(2 * t, 2)], own_sem.at[4 + j]))
        own.append(pltpu.make_async_copy(src_s.at[:, :, cols(s)], a_s.at[j, :, tokens(s)], own_sem.at[7 + j]))
    pl.semaphore_wait(barrier, 1 + t + 2 * half_z + x)
    for d in y_others:
        signal_if(d < t, ready_y, tm=d)
    for d in (far, cross):
        signal_if(half_z == 1, ready_z, space=d)
    for k, d in zip(x_index, x_others):
        signal_if(k < x, ready_x, rep=d)

    block = part // 2 // PIECES
    quarter = block // n

    def weight_block(p):
        return pl.ds(pl.multiple_of((2 * p + core_id) * block, block), block)

    def weight_quarter(p):
        return pl.ds(pl.multiple_of((2 * p + core_id) * block + x * quarter, quarter), quarter)

    def weights_y(p):
        remote(wt.at[weight_quarter(p)], w_p.at[weight_quarter(p)], wy_sem.at[p], tm=mate).start()

    def weights_x(p):
        ref = w_p.at[weight_quarter(p)]
        arrived(ref, wy_sem.at[p])
        for d in x_others:
            remote(ref, ref, wx_sem.at[p], rep=d).start()

    def weights_c(p):
        arrived(w_p.at[pl.ds(0, 3 * quarter)], wx_sem.at[p])
        ref = w_p.at[weight_block(p)]
        remote(ref, ref, wc_sem.at[p], space=pair).start()

    def weights_here(p):
        arrived(w_p.at[pl.ds(0, block)], wc_sem.at[p])

    def send_space(f):
        for d, slot in ((far, 0), (pair, 1)):
            remote(up.at[f], up_s.at[f, tokens(s)], upz_sem.at[f, slot], space=d).start()
        for j, src in enumerate((qs, ks, vs)):
            for d in (far, cross, pair):
                remote(src.at[f, :, cols(d)], a_s.at[j, f, tokens(s)], qkvz_sem.at[f], space=d).start()

    def pass_space(f):
        arrived(up_s.at[f, pl.ds(0, rows)], upz_sem.at[f, 0])
        remote(up_s.at[f, tokens(far)], up_s.at[f, tokens(far)], upz_sem.at[f, 2], space=pair).start()

    def finish_space(f):
        arrived(up_s.at[f, pl.ds(0, rows)], upz_sem.at[f, 1])
        arrived(up_s.at[f, pl.ds(0, rows)], upz_sem.at[f, 2])
        arrived(a_s.at[:, f, pl.ds(0, 3 * rows)], qkvz_sem.at[f])

    def send_time(i):
        for j, src in enumerate((qt, kt, vt)):
            for d in (y_up, y_down, y_far):
                remote(src.at[:, toks(i), cols(d)], a_t.at[j, pl.ds(2 * t, 2), toks(i)], qkvy_sem.at[i], tm=d).start()

    def time_arrived(i):
        arrived(a_t.at[:, pl.ds(0, 6), toks(i)], qkvy_sem.at[i])

    def project_own():
        og = mul(up_t[...].reshape(4 * rows, width), w_t[...], NT).astype(jnp.bfloat16).reshape(4, rows, part)
        og_t[pl.ds(2 * t, 2)] = og[:2]
        og_t[pl.ds(2 * mirror, 2)] = og[2:]

    def project_mate():
        og_p[...] = mul(up_t[...].reshape(4 * rows, width), w_p[...], NT).astype(jnp.bfloat16).reshape(4, rows, part)
        for i in range(steps):
            for k, d in ((0, t), (2, mirror)):
                remote(og_p.at[pl.ds(k, 2), toks(i)], og_t.at[pl.ds(2 * d, 2), toks(i)], ogy_sem.at[i], tm=mate).start()

    def time_step(i):
        size = 8 * STEP
        mask = (lax.broadcasted_iota(jnp.int32, (size, size), 0) % STEP
                == lax.broadcasted_iota(jnp.int32, (size, size), 1) % STEP)
        for h in range(heads):
            c = slice(h * HEAD, (h + 1) * HEAD)
            q, k, v = (a_t[j, :, toks(i), c].reshape(size, HEAD) for j in range(3))
            o = og_t[:, toks(i), c].reshape(size, HEAD)
            for j, g in enumerate(attention(q, k, v, o, mask)):
                g_t[j, :, toks(i), c] = g.reshape(8, STEP, HEAD)
        for d in (y_far, y_up, y_down):
            remote(g_t.at[:, pl.ds(2 * d, 2), toks(i)], out.at[pl.ds(3, 3), :, toks(i), cols(t)], gy_sem.at[0], tm=d).start()
        pltpu.make_async_copy(g_t.at[:, pl.ds(2 * t, 2), toks(i)], out.at[pl.ds(3, 3), :, toks(i), cols(t)], gy_sem.at[1]).start()

    def space_part(f):
        og_s[...] = mul(up_s[f], w_s[...], NT).astype(jnp.bfloat16)

        def head(h, carry):
            c = pl.ds(pl.multiple_of(h * HEAD, HEAD), HEAD)
            q, k, v = (a_s[j, f, :, c] for j in range(3))
            for j, g in enumerate(attention(q, k, v, og_s[:, c], None)):
                g_s[j, f, :, c] = g
            return carry

        half = heads // 2
        for b in range(2):
            lax.fori_loop(b * half, (b + 1) * half, head, 0)
            here = pl.ds(b * half * HEAD, half * HEAD)
            there = pl.ds(pl.multiple_of(s * part + b * half * HEAD, HEAD), half * HEAD)
            for d in (far, cross, pair):
                remote(g_s.at[:, f, tokens(d), here], out.at[pl.ds(0, 3), f, :, there], gz_sem.at[0], space=d).start()
            pltpu.make_async_copy(g_s.at[:, f, tokens(s), here], out.at[pl.ds(0, 3), f, :, there], gz_sem.at[1]).start()

    @pl.when(half_z == 1)
    def _():
        send_space(0)

    @pl.when(t < n - 1)
    def _():
        pl.semaphore_wait(ready_y, n - 1 - t)

    for p in range(PIECES):
        weights_y(p)
    remote(up, up_t.at[pl.ds(2, 2)], upy_sem.at[0], tm=mirror).start()
    send_time(0)
    send_time(1)

    @pl.when(half_z == 0)
    def _():
        pl.semaphore_wait(ready_z, 2)
        send_space(0)

    for copy in own:
        copy.start()

    @pl.when(x < n - 1)
    def _():
        pl.semaphore_wait(ready_x, n - 1 - x)

    for copy in own:
        copy.wait()
    for p in range(PIECES):
        weights_x(p)
    send_time(2)
    send_time(3)
    pass_space(0)
    send_space(1)
    for p in range(PIECES):
        weights_c(p)
    send_time(4)
    send_time(5)
    arrived(up_t.at[pl.ds(2, 2)], upy_sem.at[0])
    project_own()
    for p in range(PIECES):
        weights_here(p)
    project_mate()
    finish_space(0)
    space_part(0)

    def step(i, carry):
        time_arrived(i)
        arrived(og_t.at[pl.ds(0, 4), toks(i)], ogy_sem.at[i])
        time_step(i)

        @pl.when(i == SPATIAL_AFTER)
        def _():
            pass_space(1)
            finish_space(1)
            space_part(1)
        return carry

    lax.fori_loop(0, steps, step, 0)

    arrived(out.at[pl.ds(0, 3), :, :, pl.ds(0, part)], gz_sem.at[1])
    arrived(out.at[pl.ds(0, 3), :, :, pl.ds(0, 3 * part)], gz_sem.at[0])
    arrived(out.at[pl.ds(3, 3), :, :, pl.ds(0, part)], gy_sem.at[1])
    arrived(out.at[pl.ds(3, 3), :, :, pl.ds(0, 3 * part)], gy_sem.at[0])
    arrived(w_p, send_sem.at[0])
    for _ in range(4):
        arrived(up_t.at[pl.ds(0, 2)], send_sem.at[0])
    arrived(og_p, send_sem.at[0])
    for ref in (a_s.at[:, :, pl.ds(0, 3 * rows)], a_t.at[:, pl.ds(0, 6)]):
        arrived(ref, send_sem.at[0])
        arrived(ref, send_sem.at[0])


def local(*args):
    up, ws = args[6], args[7]
    frames, rows, width = up.shape
    part = ws.shape[0]
    bf = jnp.bfloat16
    anywhere = pl.BlockSpec(memory_space=pl.ANY)
    whole = pl.pallas_call(
        core,
        out_shape=pltpu.VMEM((6, frames, rows, width), bf),
        in_specs=[pl.BlockSpec(memory_space=pltpu.HBM)] * 9,
        out_specs=pl.BlockSpec(memory_space=pltpu.VMEM),
        scratch_shapes=[
            pltpu.VMEM((frames, 4 * rows, width), bf),
            pltpu.VMEM((2 * frames, rows, width), bf),
            pltpu.VMEM((3, frames, 4 * rows, part), bf),
            pltpu.VMEM((3, 4 * frames, rows, part), bf),
            pltpu.VMEM((part, width), bf),
            pltpu.VMEM((part, width), bf),
            pltpu.VMEM((part, width), bf),
            pltpu.VMEM((4 * rows, part), bf),
            pltpu.VMEM((4 * frames, rows, part), bf),
            pltpu.VMEM((2 * frames, rows, part), bf),
            pltpu.VMEM((3, frames, 4 * rows, part), bf),
            pltpu.VMEM((3, 4 * frames, rows, part), bf),
            pltpu.SemaphoreType.DMA((10,)),
            pltpu.SemaphoreType.DMA((frames, 3)),
            pltpu.SemaphoreType.DMA((frames,)),
            pltpu.SemaphoreType.DMA((1,)),
            pltpu.SemaphoreType.DMA((rows // STEP,)),
            pltpu.SemaphoreType.DMA((rows // STEP,)),
            pltpu.SemaphoreType.DMA((PIECES,)),
            pltpu.SemaphoreType.DMA((PIECES,)),
            pltpu.SemaphoreType.DMA((PIECES,)),
            pltpu.SemaphoreType.DMA((2,)),
            pltpu.SemaphoreType.DMA((2,)),
            pltpu.SemaphoreType.DMA((1,)),
            pltpu.SemaphoreType.REGULAR,
            pltpu.SemaphoreType.REGULAR,
            pltpu.SemaphoreType.REGULAR,
        ],
        compiler_params=pltpu.CompilerParams(
            collective_id=0, has_side_effects=True, vmem_limit_bytes=57 * 1024 * 1024),
        name="core",
    )(*args)
    return tuple(whole[j] for j in range(6))


def solution(mesh):
    rows = P(("rep", "tm"), "space", None)
    in_specs = (rows,) * 7 + (P("space", None), P("tm", None))
    return jax.shard_map(local, mesh=mesh, in_specs=in_specs, out_specs=(rows,) * 6, check_vma=False)
```
